32 devices in a mesh: dom: 32 (over z, y, x, core).
Axes of the slice: x: 2, y: 2, z: 4, core: 2. Of those that a mesh axis runs over, the one named last changes fastest.
Arguments:
- right_side: float32 [512, 320], P('dom'), may hold values from -6 to 6
- start_state: float32 [512, 320], P('dom'), may hold values from -6 to 6
- pivot_inverse: bfloat16 [512, 320, 320], P('dom')
- lower_block: bfloat16 [512, 320, 320], P('dom'), may hold values from -0.15625 to 0.15625
- upper_block: bfloat16 [512, 320, 320], P('dom'), may hold values from -0.15625 to 0.15625
- face_blocks: bfloat16 [512, 4, 320, 320], P('dom'), may hold values from -0.15625 to 0.15625
- neighbours: int32 [4, 512], P(None, 'dom'), may hold values from -1 to 511, as said below
- element_slot: int32 [512], P('dom'), may hold values from 0 to 1023, as said below
Outputs:
- new_state: float32 [512, 320], P('dom')
The draws below stay inside these ranges and needn't reach their ends.
Inputs may be any that keep to these rules, and one draw needn't show every extreme that they name: `neighbours`: an entry -1 marks a boundary face; any other entry n of element e satisfies |n // 16 - e // 16| <= 1. Distinct elements have distinct values. The owner element_slot[e] // 32 differs from e // 16 by at most one. At most 8 elements of one partition have the owner below it and at most 8 the owner above it; in every draw some partition sends 8 each way, and some owner has all 32 slots taken.
All inputs are finite; a program needn't handle non-finite values.
Results may differ from the reference program's by a relative error of at most 0.0095.
Values may be sent and summed in bfloat16 or wider, within the bound.
No kernel may reach another device: no remote copies, remote signals or barrier semaphores. Data moves between devices by JAX's collectives and lax.ppermute only.
A program may use at most 128 MiB of HBM per device.

```python
import jax
import jax.numpy as jnp
from jax import lax

NV = 320
E_DEV = 16
FACES = 4
LMAX = 8
SWEEPS = 2
SLOTS = 32
ROWS = 4
ELEMENTS = 512
N_DOM = 32


def draw_pivot_inverse(key, part):
    key = jax.random.fold_in(key, 5)
    first_key, second_key = jax.random.split(key, 2)
    shape = (E_DEV * N_DOM, NV, NV)
    identity = (jnp.arange(NV)[:, None] == jnp.arange(NV)[None, :]).astype(jnp.float32)
    spread = jax.random.normal(first_key, shape, jnp.float32) * 0.5 * NV ** (-0.5)
    diagonal = jax.random.uniform(second_key, (E_DEV * N_DOM, NV), jnp.float32, 0.6, 1.4)
    return (spread + identity[None, :, :] * diagonal[:, :, None]).astype(jnp.bfloat16)


def draw_neighbours(key, part):
    key = jax.random.fold_in(key, 9)
    keys = jax.random.split(key, 3)
    elements = E_DEV * N_DOM
    home = jnp.arange(elements, dtype=jnp.int32)[:, None] // E_DEV
    offset = jax.random.randint(keys[0], (elements, FACES), -1, 2)
    target = jnp.clip(home + offset, 0, N_DOM - 1)
    within = jax.random.randint(keys[1], (elements, FACES), 0, E_DEV)
    identity_ids = target * E_DEV + within
    boundary = jax.random.randint(keys[2], (elements, FACES), 0, 8) == 0
    identity_ids = jnp.where(boundary, -1, identity_ids)
    identity_ids = identity_ids.at[0, FACES - 1].set(-1)
    identity_ids = identity_ids.at[elements - 2, 0].set(elements - 1)
    return identity_ids.T.astype(jnp.int32)


def permute_rows(row_key, length):
    return jax.random.permutation(row_key, length)


def draw_element_slot(key, part):
    key = jax.random.fold_in(key, 7)
    keys = jax.random.split(key, 5)
    devices = N_DOM
    bucket = E_DEV // 2
    slot_count = 2 * E_DEV
    device_ids = jnp.arange(devices, dtype=jnp.int32)
    to_down = jax.random.randint(keys[0], (devices,), 0, bucket + 1)
    to_up = jax.random.randint(keys[1], (devices,), 0, bucket + 1)
    to_down = jnp.where(device_ids == 0, 0, to_down)
    to_up = jnp.where(device_ids == devices - 1, 0, to_up)
    corner = jax.random.randint(keys[2], (), 1, devices - 2)
    to_down = jnp.where(device_ids == corner, bucket, to_down)
    to_up = jnp.where(device_ids == corner, bucket, to_up)
    to_down = jnp.where(device_ids == corner + 1, 0, to_down)
    to_up = jnp.where(device_ids == corner + 1, 0, to_up)
    to_down = jnp.where(device_ids == corner + 2, bucket, to_down)
    staying = E_DEV - to_down - to_up
    orders = jax.vmap(lambda row_key: permute_rows(row_key, E_DEV))(jax.random.split(keys[3], devices))
    ranking = jnp.argsort(orders, axis=1, stable=True).astype(jnp.int32)
    down_count = to_down[:, None]
    up_count = to_up[:, None]
    offset = jnp.where(ranking < down_count, -1, jnp.where(ranking < down_count + up_count, 1, 0))
    owner = device_ids[:, None] + offset
    up_before = jnp.concatenate([jnp.zeros((1,), jnp.int32), to_up[:-1].astype(jnp.int32)])
    place = jnp.where(offset == 1, ranking - down_count, jnp.where(offset == 0, up_before[:, None] + ranking - down_count - up_count, up_before[owner] + staying[owner] + ranking))
    slot_orders = jax.vmap(lambda row_key: permute_rows(row_key, slot_count))(jax.random.split(keys[4], devices)).astype(jnp.int32)
    first_target = jnp.where(device_ids == 0, 0, slot_count - 1).astype(jnp.int32)
    slot_orders = (slot_orders - slot_orders[:, :1] + first_target[:, None] + 2 * slot_count) % slot_count
    chosen = slot_orders[owner, place]
    return (owner * slot_count + chosen).reshape(-1).astype(jnp.int32)


def levels(own_key, dims, cuts, low, high):
    level = 1.0
    for axis_at, parts in cuts:
        draws = jax.random.uniform(jax.random.fold_in(jax.random.fold_in(own_key, 6), axis_at), (parts,), jnp.float32, low / len(cuts), high / len(cuts))
        level = level * jnp.repeat(jnp.exp(draws), dims[axis_at] // parts).reshape((-1,) + (1,) * (len(dims) - 1 - axis_at))
    return level


def normal_values(key, dims, deviation, reach, pieces=(), held_as=jnp.bfloat16):
    result = jax.random.normal(key, dims, jnp.float32) * deviation
    if len(pieces) > 0:
        result = levels(key, dims, pieces, -0.22, 0.18) * result
    return jnp.clip(result, min=-reach, max=reach).astype(held_as)


def setup_inputs(seed: int = 0) -> dict:
    streams_of = jax.random.split(jax.random.key(seed), 9)
    right_side = normal_values(streams_of[0], (ELEMENTS, NV), 1.0, 6.0, ((0, 32),), jnp.float32)
    start_state = normal_values(streams_of[1], (ELEMENTS, NV), 1.0, 6.0, ((0, 32),), jnp.float32)
    pivot_inverse = draw_pivot_inverse(jax.random.fold_in(streams_of[8], 71), 0)
    lower_block = normal_values(streams_of[3], (ELEMENTS, NV, NV), (4 * NV) ** -0.5, 0.15625, ((0, 32),))
    upper_block = normal_values(streams_of[4], (ELEMENTS, NV, NV), (4 * NV) ** -0.5, 0.15625, ((0, 32),))
    face_blocks = normal_values(streams_of[5], (ELEMENTS, FACES, NV, NV), (4 * NV) ** -0.5, 0.15625, ((0, 32),))
    neighbours = draw_neighbours(jax.random.fold_in(streams_of[8], 71), 0)
    element_slot = draw_element_slot(jax.random.fold_in(streams_of[8], 71), 0)
    return dict(right_side=right_side, start_state=start_state, pivot_inverse=pivot_inverse, lower_block=lower_block, upper_block=upper_block, face_blocks=face_blocks, neighbours=neighbours, element_slot=element_slot)


def premultiply(pair):
    pivot, coupling = pair
    return jnp.einsum('eij,ejk->eik', pivot.astype(jnp.float32), coupling.astype(jnp.float32)).astype(jnp.bfloat16)


def face_term(pair):
    blocks, states = pair
    return jnp.einsum('efij,efj->ei', blocks.astype(jnp.float32), states.astype(jnp.float32))


def pivot_apply(pair):
    blocks, states = pair
    return jnp.einsum('eij,ej->ei', blocks.astype(jnp.float32), states.astype(jnp.float32))


def reference(right_side, start_state, pivot_inverse, lower_block, upper_block, face_blocks, neighbours, element_slot):
    elements = right_side.shape[0]
    square = (N_DOM, E_DEV, NV, NV)
    slot_element = jnp.full((N_DOM * SLOTS,), -1, jnp.int32).at[element_slot].set(jnp.arange(elements, dtype=jnp.int32))
    table = slot_element.reshape(N_DOM * ROWS, LMAX)
    pivots = pivot_inverse.reshape(square)
    scaled_lower = lax.map(premultiply, (pivots, lower_block.reshape(square))).reshape(elements, NV, NV)
    scaled_upper = lax.map(premultiply, (pivots, upper_block.reshape(square))).reshape(elements, NV, NV)
    across = neighbours.T
    face_live = across >= 0
    safe_index = jnp.clip(across, 0, elements - 1)
    current = start_state
    for sweep_step in range(SWEEPS):
        rounded = current.astype(jnp.bfloat16)
        gathered = jnp.where(face_live[:, :, None], rounded[safe_index], jnp.zeros((), jnp.bfloat16))
        face_sum = lax.map(face_term, (face_blocks.reshape(N_DOM, E_DEV, FACES, NV, NV), gathered.reshape(N_DOM, E_DEV, FACES, NV))).reshape(elements, NV)
        residual = (right_side - face_sum).astype(jnp.bfloat16)
        scaled = lax.map(pivot_apply, (pivots, residual.reshape(N_DOM, E_DEV, NV))).reshape(elements, NV)
        previous = jnp.zeros((N_DOM * ROWS, NV), jnp.bfloat16)
        forward = []
        for position in range(LMAX):
            column = table[:, position]
            live = (column >= 0)[:, None]
            safe_column = jnp.maximum(column, 0)
            carried = jnp.einsum('rij,rj->ri', scaled_lower[safe_column].astype(jnp.float32), previous.astype(jnp.float32))
            value = jnp.where(live, scaled[safe_column] - carried, jnp.zeros((), jnp.float32))
            forward.append(value)
            previous = value.astype(jnp.bfloat16)
        following = jnp.zeros((N_DOM * ROWS, NV), jnp.bfloat16)
        backward = [None] * LMAX
        for position in reversed(range(LMAX)):
            column = table[:, position]
            live = (column >= 0)[:, None]
            safe_column = jnp.maximum(column, 0)
            carried = jnp.einsum('rij,rj->ri', scaled_upper[safe_column].astype(jnp.float32), following.astype(jnp.float32))
            value = jnp.where(live, forward[position] - carried, jnp.zeros((), jnp.float32))
            backward[position] = value
            following = value.astype(jnp.bfloat16)
        solved = jnp.stack(backward, axis=1).reshape(N_DOM * SLOTS, NV)
        current = solved[element_slot]
    return current
```

```python
import functools

import jax
import jax.numpy as jnp
from jax import lax
from jax.experimental import pallas as pl
from jax.experimental.pallas import tpu as pltpu
from jax.sharding import PartitionSpec as P

LMAX = 8
SWEEPS = 2
WIDE = 256
ANY = pl.BlockSpec(memory_space=pl.ANY)
SMEM = pl.BlockSpec(memory_space=pltpu.SMEM)
VMEM = pl.BlockSpec(memory_space=pltpu.VMEM)
NT = (((1,), (1,)), ((), ()))


def dot_nt(a, b):
    return lax.dot_general(a, b, NT, preferred_element_type=jnp.float32)


def dot_nn(a, b):
    return jnp.dot(a, b, preferred_element_type=jnp.float32)


def pair_product(pivot, lower, upper, out):
    out[:, :WIDE] = dot_nn(pivot, lower[:, :WIDE]).astype(jnp.bfloat16)
    out[:, WIDE : 2 * WIDE] = dot_nn(pivot, upper[:, :WIDE]).astype(jnp.bfloat16)
    tails = jnp.concatenate([lower[:, WIDE:], upper[:, WIDE:]], axis=1)
    out[:, 2 * WIDE :] = dot_nn(pivot, tails).astype(jnp.bfloat16)


def outgoing_kernel(chunk, slot_count, slots, target, piv, low, upp, first, second, pb, lb, ub, stage, insem, outsem):
    bucket = stage.shape[0]
    count = jnp.int32(0)
    for e in range(slots.shape[0]):
        hit = (slots[e] // slot_count) == target[0]

        @pl.when(hit)
        def _(e=e, count=count):
            pltpu.make_async_copy(piv.at[e], pb.at[count], insem.at[0, count]).start()
            pltpu.make_async_copy(low.at[e], lb.at[count], insem.at[1, count]).start()
            pltpu.make_async_copy(upp.at[e], ub.at[count], insem.at[2, count]).start()

        count = count + hit.astype(jnp.int32)

    def sent(k):
        dest = first.at[k] if k < chunk else second.at[k - chunk]
        return pltpu.make_async_copy(stage.at[k], dest, outsem.at[k])

    for k in range(bucket):

        @pl.when(k < count)
        def _(k=k):
            pltpu.make_async_copy(piv.at[0], pb.at[k], insem.at[0, k]).wait()
            pltpu.make_async_copy(low.at[0], lb.at[k], insem.at[1, k]).wait()
            pltpu.make_async_copy(upp.at[0], ub.at[k], insem.at[2, k]).wait()
            pair_product(pb[k], lb[k], ub[k], stage.at[k])
            sent(k).start()

    for k in range(bucket):

        @pl.when(k < count)
        def _(k=k):
            sent(k).wait()


def staying_kernel(slot_count, slots, me, target, piv, low, upp, beside, own, pb, lb, ub, stage, insem, outsem):
    elems = slots.shape[0]

    def loads(e):
        return [
            pltpu.make_async_copy(src.at[e], dst.at[e], insem.at[i, e])
            for i, (src, dst) in enumerate(((piv, pb), (low, lb), (upp, ub)))
        ]

    for e in range(elems):
        owner = slots[e] // slot_count

        @pl.when((owner == me[0]) | (owner == target[0]))
        def _(e=e):
            for copy in loads(e):
                copy.start()

    def step(e, count):
        owner = slots[e] // slot_count
        across = owner == target[0]

        @pl.when((owner == me[0]) | across)
        def _():
            for copy in loads(e):
                copy.wait()
            pair_product(pb[e], lb[e], ub[e], stage.at[e])

        @pl.when(across)
        def _():
            pltpu.make_async_copy(stage.at[e], beside.at[count], outsem.at[e]).start()

        @pl.when(owner == me[0])
        def _():
            pltpu.make_async_copy(stage.at[e], own.at[e], outsem.at[e]).start()

        return count + across.astype(jnp.int32)

    lax.fori_loop(0, elems, step, jnp.int32(0))
    for e in range(elems):
        owner = slots[e] // slot_count

        @pl.when((owner == me[0]) | (owner == target[0]))
        def _(e=e):
            pltpu.make_async_copy(stage.at[e], own.at[e], outsem.at[e]).wait()


def face_kernel(counts, send_ref, index_ref, rhs_ref, *refs):
    parts = refs[: len(counts)]
    faces_ref, piv_ref, side_ref, across_ref, own_ref, rows, gathered, scaled = refs[len(counts) :]
    e = pl.program_id(0)
    elems = rhs_ref.shape[0]
    faces = faces_ref.shape[1]
    width = rhs_ref.shape[1]

    @pl.when(e == 0)
    def _():
        at = 0
        for part, size in zip(parts, counts):
            rows[at : at + size] = part[...]
            at += size
        wanted = index_ref[...] == lax.broadcasted_iota(jnp.int32, (faces * elems, at), 1)
        picked = dot_nn(wanted.astype(jnp.bfloat16), rows[...])
        gathered[...] = picked.astype(jnp.bfloat16)

    total = dot_nt(gathered[:elems], faces_ref[0, 0])
    for f in range(1, faces):
        total += dot_nt(gathered[f * elems : (f + 1) * elems], faces_ref[0, f])
    residual = (rhs_ref[...] - total).astype(jnp.bfloat16)
    applied = dot_nt(residual, piv_ref[0])
    row = lax.broadcasted_iota(jnp.int32, (elems, width), 0)
    scaled[...] = jnp.where(row == e, applied, scaled[...])

    @pl.when(e == elems - 1)
    def _():
        own_ref[...] = scaled[...]
        bucket = side_ref.shape[0]
        for k in range(bucket):
            side_ref[k : k + 1] = scaled[pl.ds(send_ref[k], 1), :]
            across_ref[k : k + 1] = scaled[pl.ds(send_ref[bucket + k], 1), :]


def solve_kernel(last, chunk, table, back, side_m, own_m, first_m, second_m, side_s, own_s, across_s, *refs):
    outs = refs[:3] if last else refs[:1]
    mats, items, ahead, behind, sems = refs[len(outs) :]
    bucket = side_s.shape[0]
    elems = own_s.shape[0]
    width = own_s.shape[1]
    lines = table.shape[0] // LMAX
    tail = width - WIDE

    def load(p, r):
        slot = r * LMAX + p
        at = p * lines + r
        item = table[slot]
        sources = (
            (side_m, 0, bucket),
            (own_m, bucket, bucket + elems),
            (first_m, bucket + elems, bucket + elems + chunk),
            (second_m, bucket + elems + chunk, 2 * bucket + elems),
        )
        for source, low, high in sources:

            @pl.when((item >= low) & (item < high))
            def _(source=source, low=low):
                pltpu.make_async_copy(source.at[item - low], mats.at[at], sems.at[at]).start()

    for p in range(LMAX):
        for r in range(lines):
            load(p, r)

    items[:bucket] = side_s[...]
    items[bucket : bucket + elems] = own_s[...]
    items[bucket + elems :] = across_s[...]
    sublanes = ahead.shape[1]
    row = lax.broadcasted_iota(jnp.int32, (sublanes, width), 0)
    zeros = jnp.zeros((sublanes, tail), jnp.bfloat16)

    def sweep_step(p, x, half):
        lead = x[:, :WIDE]
        ends = [x[:, WIDE:], zeros] if half == 0 else [zeros, x[:, WIDE:]]
        ending = jnp.concatenate(ends, axis=1)
        carried = jnp.zeros((sublanes, width), jnp.float32)
        for r in range(lines):
            at = p * lines + r
            got = dot_nt(lead, mats[at, :, half * WIDE : (half + 1) * WIDE])
            got += dot_nt(ending, mats[at, :, 2 * WIDE :])
            live = table[r * LMAX + p] >= 0
            carried = jnp.where((row == r) & live, got, carried)
        return carried

    for p in range(LMAX):
        ahead[p] = jnp.zeros((sublanes, width), jnp.float32)
        for r in range(lines):
            item = table[r * LMAX + p]

            @pl.when(item >= 0)
            def _(p=p, r=r, item=item):
                ahead[p, r : r + 1, :] = items[pl.ds(item, 1), :]

    x = None
    for p in range(LMAX):
        for r in range(lines):

            @pl.when(table[r * LMAX + p] >= 0)
            def _(p=p, r=r):
                at = p * lines + r
                pltpu.make_async_copy(own_m.at[0], mats.at[at], sems.at[at]).wait()

        value = ahead[p]
        if p > 0:
            value = value - sweep_step(p, x, 0)
            ahead[p] = value
        x = value.astype(jnp.bfloat16)
    x = None
    for p in reversed(range(LMAX)):
        value = ahead[p]
        if p < LMAX - 1:
            value = value - sweep_step(p, x, 1)
        behind[p] = value
        x = value.astype(jnp.bfloat16)
    if last:
        at = 0
        for out in outs:
            for k in range(out.shape[0]):
                slot = back[at + k]
                out[k : k + 1] = behind[slot % LMAX, pl.ds(slot // LMAX, 1), :]
            at += out.shape[0]
    else:
        (out,) = outs
        for p in range(LMAX):
            items[p * lines : (p + 1) * lines] = behind[p, :lines, :]
        out[...] = items[...].astype(jnp.bfloat16)


def place_kernel(index, side, own, across, out, items):
    bucket = side.shape[0]
    elems = own.shape[0]
    items[:bucket] = side[...]
    items[bucket : bucket + elems] = own[...]
    items[bucket + elems :] = across[...]
    for e in range(elems):
        out[e : e + 1] = items[pl.ds(index[e], 1), :]


def pack_order(selected, bucket):
    members = jnp.arange(selected.shape[0], dtype=jnp.int32)
    before = (members[None, :] <= members[:, None]) & selected[None, :]
    ordering = jnp.sum(before.astype(jnp.int32), axis=1) - 1
    positions = jnp.arange(bucket, dtype=jnp.int32)[:, None]
    matches = selected[None, :] & (ordering[None, :] == positions)
    picked = jnp.sum(jnp.where(matches, members[None, :], 0), axis=1)
    return (picked, jnp.any(matches, axis=1), jnp.clip(ordering, 0, bucket - 1))


def body(
    chunk,
    right_side,
    start_state,
    pivot_inverse,
    lower_block,
    upper_block,
    face_blocks,
    neighbours,
    element_slot,
):
    elems, width = right_side.shape
    faces = face_blocks.shape[1]
    bucket = elems // 2
    slot_count = 2 * elems
    lines = slot_count // LMAX
    packed = 2 * width
    devices = lax.axis_size("dom")
    me = lax.axis_index("dom").astype(jnp.int32)
    odd = me % 2 == 1
    side = jnp.where(odd, me - 1, me + 1)
    across = jnp.where(odd, me + 1, me - 1)
    side_pairs = [(i, i ^ 1) for i in range(devices)]
    across_pairs = [(i, i + 1) for i in range(1, devices - 1, 2)]
    across_pairs = across_pairs + [(j, i) for i, j in across_pairs]

    def to_side(array):
        return lax.ppermute(array, "dom", side_pairs)

    def to_across(array):
        return lax.ppermute(array, "dom", across_pairs)

    f32, bf16 = jnp.float32, jnp.bfloat16
    block = (width, width)
    pair = (width, packed)
    dma = pltpu.SemaphoreType.DMA

    first, second = pl.pallas_call(
        functools.partial(outgoing_kernel, chunk, slot_count),
        out_shape=[
            jax.ShapeDtypeStruct((chunk,) + pair, bf16),
            jax.ShapeDtypeStruct((bucket - chunk,) + pair, bf16),
        ],
        in_specs=[SMEM, SMEM, ANY, ANY, ANY],
        out_specs=[ANY, ANY],
        scratch_shapes=[pltpu.VMEM((bucket,) + block, bf16)] * 3
        + [pltpu.VMEM((bucket,) + pair, bf16), dma((3, bucket)), dma((bucket,))],
        compiler_params=pltpu.CompilerParams(vmem_limit_bytes=40 << 20),
        name="outgoing",
    )(element_slot, across[None], pivot_inverse, lower_block, upper_block)
    first_in = to_across(first)
    rounded = start_state.astype(bf16)
    state_across = to_across(rounded)
    slot_across = to_across(element_slot)
    second_in = to_across(second)
    state_side = to_side(rounded)
    slot_side = to_side(element_slot)

    side_pack, own_pack = pl.pallas_call(
        functools.partial(staying_kernel, slot_count),
        out_shape=[
            jax.ShapeDtypeStruct((bucket,) + pair, bf16),
            jax.ShapeDtypeStruct((elems,) + pair, bf16),
        ],
        in_specs=[SMEM, SMEM, SMEM, ANY, ANY, ANY],
        out_specs=[ANY, ANY],
        scratch_shapes=[pltpu.VMEM((elems,) + block, bf16)] * 3
        + [pltpu.VMEM((elems,) + pair, bf16), dma((3, elems)), dma((elems,))],
        compiler_params=pltpu.CompilerParams(vmem_limit_bytes=40 << 20),
        name="staying",
    )(element_slot, me[None], side[None], pivot_inverse, lower_block, upper_block)
    side_in = to_side(side_pack)

    owner = element_slot // slot_count
    side_index, _, side_rank = pack_order(owner == side, bucket)
    across_index, _, across_rank = pack_order(owner == across, bucket)
    send_index = jnp.concatenate([side_index, across_index])
    spread = jnp.arange(elems, dtype=jnp.int32)
    item_of_own = jnp.where(
        owner == me,
        bucket + spread,
        jnp.where(owner == side, side_rank, bucket + elems + across_rank),
    )
    across_live = (across >= 0) & (across < devices)
    in_side, in_side_valid, _ = pack_order(slot_side // slot_count == me, bucket)
    in_across, in_across_valid, _ = pack_order((slot_across // slot_count == me) & across_live, bucket)
    item_slot = jnp.concatenate(
        [
            jnp.where(in_side_valid, slot_side[in_side] % slot_count, -1),
            jnp.where(owner == me, element_slot % slot_count, -1),
            jnp.where(in_across_valid, slot_across[in_across] % slot_count, -1),
        ]
    )
    everything = jnp.arange(slot_count, dtype=jnp.int32)
    slot_matches = item_slot[None, :] == everything[:, None]
    table = jnp.max(jnp.where(slot_matches, everything[None, :], -1), axis=1)
    back = jnp.maximum(item_slot, 0)

    home = neighbours // elems
    within = neighbours % elems
    near = jnp.where(home == me, elems, jnp.where(home == side, 0, 2 * elems)) + within
    near = jnp.where(neighbours >= 0, near, -1)
    all_slots = jnp.concatenate([slot_side, element_slot, slot_across])
    place = all_slots[jnp.maximum(near, 0)]
    place_owner = place // slot_count
    place_slot = place % slot_count
    place_row = (place_slot % LMAX) * lines + place_slot // LMAX
    across_chip = across // 2
    far = jnp.where(
        place_owner == me,
        0,
        jnp.where(
            place_owner == side,
            slot_count,
            jnp.where(place_owner // 2 == across_chip, 2 * slot_count, 4 * slot_count)
            + (place_owner % 2) * slot_count,
        ),
    )
    far = jnp.where(neighbours >= 0, far + place_row, -1)

    def face_part(index, parts):
        counts = tuple(part.shape[0] for part in parts)
        whole = lambda *shape: pl.BlockSpec(shape, lambda e: (0,) * len(shape))
        return pl.pallas_call(
            functools.partial(face_kernel, counts),
            grid=(elems,),
            out_shape=[
                jax.ShapeDtypeStruct((bucket, width), f32),
                jax.ShapeDtypeStruct((bucket, width), f32),
                jax.ShapeDtypeStruct((elems, width), f32),
            ],
            in_specs=[SMEM, whole(faces * elems, 1), whole(elems, width)]
            + [whole(count, width) for count in counts]
            + [
                pl.BlockSpec((1, faces, width, width), lambda e: (e, 0, 0, 0)),
                pl.BlockSpec((1, width, width), lambda e: (e, 0, 0)),
            ],
            out_specs=[whole(bucket, width), whole(bucket, width), whole(elems, width)],
            scratch_shapes=[
                pltpu.VMEM((sum(counts), width), bf16),
                pltpu.VMEM((faces * elems, width), bf16),
                pltpu.VMEM((elems, width), f32),
            ],
            compiler_params=pltpu.CompilerParams(vmem_limit_bytes=40 << 20),
            name="faces",
        )(send_index, index.reshape(-1, 1), right_side, *parts, face_blocks, pivot_inverse)

    def solve(last, side_s, own_s, across_s):
        if last:
            shapes = [(bucket, width), (elems, width), (bucket, width)]
            out_shape = [jax.ShapeDtypeStruct(shape, f32) for shape in shapes]
        else:
            out_shape = [jax.ShapeDtypeStruct((slot_count, width), bf16)]
        return pl.pallas_call(
            functools.partial(solve_kernel, last, chunk),
            out_shape=out_shape,
            in_specs=[SMEM, SMEM, ANY, ANY, ANY, ANY, VMEM, VMEM, VMEM],
            out_specs=[VMEM] * len(out_shape),
            scratch_shapes=[
                pltpu.VMEM((slot_count,) + pair, bf16),
                pltpu.VMEM((slot_count, width), f32),
                pltpu.VMEM((LMAX, 8, width), f32),
                pltpu.VMEM((LMAX, 8, width), f32),
                dma((slot_count,)),
            ],
            compiler_params=pltpu.CompilerParams(vmem_limit_bytes=40 << 20),
            name="solve",
        )(table, back, side_in, own_pack, first_in, second_in, side_s, own_s, across_s)

    index, parts = near, [state_side, rounded, state_across]
    for sweep in range(SWEEPS):
        scaled_side, scaled_across, scaled_own = face_part(index, parts)
        got_across = to_across(scaled_across)
        got_side = to_side(scaled_side)
        solved = solve(sweep == SWEEPS - 1, got_side, scaled_own, got_across)
        if sweep < SWEEPS - 1:
            (mine,) = solved
            beside = to_side(mine)
            chip = jnp.where(
                odd, jnp.concatenate([beside, mine]), jnp.concatenate([mine, beside])
            )
            over = to_across(chip)
            under = to_side(over)
            index, parts = far, [mine, beside, over, under]
    back_side, back_own, back_across = solved
    back_across = to_across(back_across)
    back_side = to_side(back_side)
    return pl.pallas_call(
        place_kernel,
        out_shape=jax.ShapeDtypeStruct((elems, width), f32),
        in_specs=[SMEM, VMEM, VMEM, VMEM],
        out_specs=VMEM,
        scratch_shapes=[pltpu.VMEM((slot_count, width), f32)],
        name="place",
    )(item_of_own, back_side, back_own, back_across)


def solution(mesh):
    placed = (
        P("dom", None),
        P("dom", None),
        P("dom", None, None),
        P("dom", None, None),
        P("dom", None, None),
        P("dom", None, None, None),
        P(None, "dom"),
        P("dom"),
    )
    return jax.shard_map(
        functools.partial(body, 2), mesh=mesh, in_specs=placed, out_specs=P("dom", None), check_vma=False
    )
```

```python
import functools

import jax
import jax.numpy as jnp
from jax import lax
from jax.experimental import pallas as pl
from jax.experimental.pallas import tpu as pltpu
from jax.sharding import PartitionSpec as P

LMAX = 8
SWEEPS = 2
WIDE = 256
HBM = pl.BlockSpec(memory_space=pltpu.HBM)
SMEM = pl.BlockSpec(memory_space=pltpu.SMEM)
VMEM = pl.BlockSpec(memory_space=pltpu.VMEM)
ROOMY = pltpu.CompilerParams(vmem_limit_bytes=57 << 20)
FACING = pltpu.CompilerParams(vmem_limit_bytes=50 << 20)
SNUG = pltpu.CompilerParams(vmem_limit_bytes=52 << 20)
SMALL = pl.CostEstimate(flops=1 << 20, bytes_accessed=1 << 20, transcendentals=0)
NT = (((1,), (1,)), ((), ()))


def dot_nt(a, b):
    return lax.dot_general(a, b, NT, preferred_element_type=jnp.float32)


def dot_nn(a, b):
    return jnp.dot(a, b, preferred_element_type=jnp.float32)


def pair_product(pivot, lower, upper, out):
    both = jnp.concatenate([lower.T, upper.T], axis=0)
    got = dot_nt(both, pivot).astype(jnp.bfloat16)
    width = pivot.shape[0]
    out[:, :WIDE] = got[:width, :WIDE]
    out[:, WIDE : 2 * WIDE] = got[width:, :WIDE]
    out[:, 2 * WIDE :] = jnp.concatenate([got[:width, WIDE:], got[width:, WIDE:]], axis=1)


def outgoing_kernel(slot_count, slots, targets, piv, low, upp, over_out, side_out, pb, lb, ub, stage, insem, outsem):
    bucket = over_out.shape[0]
    counts = []
    for which in range(2):
        count = jnp.int32(which * bucket)
        for e in range(slots.shape[0]):
            hit = (slots[e] // slot_count) == targets[which]

            @pl.when(hit)
            def _(e=e, count=count):
                pltpu.make_async_copy(piv.at[e], pb.at[count], insem.at[0, count]).start()
                pltpu.make_async_copy(low.at[e], lb.at[count], insem.at[1, count]).start()
                pltpu.make_async_copy(upp.at[e], ub.at[count], insem.at[2, count]).start()

            count = count + hit.astype(jnp.int32)
        counts.append(count)
    for which, out in enumerate((over_out, side_out)):
        first = which * bucket

        def step(k, carry, out=out, first=first):
            pltpu.make_async_copy(piv.at[0], pb.at[k], insem.at[0, k]).wait()
            pltpu.make_async_copy(low.at[0], lb.at[k], insem.at[1, k]).wait()
            pltpu.make_async_copy(upp.at[0], ub.at[k], insem.at[2, k]).wait()
            pair_product(pb[k], lb[k], ub[k], stage.at[k])
            pltpu.make_async_copy(stage.at[k], out.at[k - first], outsem.at[k]).start()
            return carry

        lax.fori_loop(first, counts[which], step, 0)
    for which, out in enumerate((over_out, side_out)):
        first = which * bucket

        def drain(k, carry, out=out, first=first):
            pltpu.make_async_copy(stage.at[k], out.at[k - first], outsem.at[k]).wait()
            return carry

        lax.fori_loop(first, counts[which], drain, 0)


def staying_kernel(slot_count, slots, me, piv, low, upp, own, pb, lb, ub, stage, insem, outsem):
    elems = slots.shape[0]

    def loads(e):
        return [
            pltpu.make_async_copy(src.at[e], dst.at[e], insem.at[i, e])
            for i, (src, dst) in enumerate(((piv, pb), (low, lb), (upp, ub)))
        ]

    def send(e):
        return pltpu.make_async_copy(stage.at[e], own.at[e], outsem.at[e])

    for e in range(elems):

        @pl.when(slots[e] // slot_count == me[0])
        def _(e=e):
            for copy in loads(e):
                copy.start()

    def step(e, carry):
        @pl.when(slots[e] // slot_count == me[0])
        def _():
            for copy in loads(e):
                copy.wait()
            pair_product(pb[e], lb[e], ub[e], stage.at[e])
            send(e).start()

        return carry

    lax.fori_loop(0, elems, step, 0)
    for e in range(elems):

        @pl.when(slots[e] // slot_count == me[0])
        def _(e=e):
            send(e).wait()


def face_kernel(counts, send, index, rhs, *refs):
    parts = refs[: len(counts)]
    faces, piv, side_out, across_out, own_out, rows, gathered, held, scaled, fb, pb, fsem, psem = refs[len(counts) :]
    elems, width = rhs.shape
    count = faces.shape[1]
    face_copies = [pltpu.make_async_copy(faces.at[e], fb.at[e], fsem.at[e]) for e in range(elems)]
    piv_copies = [pltpu.make_async_copy(piv.at[e], pb.at[e], psem.at[e]) for e in range(elems)]
    for face_copy, piv_copy in zip(face_copies, piv_copies):
        face_copy.start()
        piv_copy.start()
    at = 0
    for part, size in zip(parts, counts):
        rows[at : at + size] = part[...]
        at += size
    wanted = index[...] == lax.broadcasted_iota(jnp.int32, (count * elems, at), 1)
    picked = dot_nn(wanted.astype(jnp.bfloat16), rows[...]).astype(jnp.bfloat16)
    gathered[...] = picked
    ends = jnp.concatenate([picked[f * elems : (f + 1) * elems, WIDE:] for f in range(count)], axis=1)
    row = lax.broadcasted_iota(jnp.int32, (elems, width), 0)

    def residual(e):
        pltpu.make_async_copy(faces.at[e], fb.at[e], fsem.at[e]).wait()
        total = dot_nt(gathered[:elems, :WIDE], fb[e, 0, :, :WIDE])
        for f in range(1, count):
            total += dot_nt(gathered[f * elems : (f + 1) * elems, :WIDE], fb[e, f, :, :WIDE])
        tails = jnp.concatenate([fb[e, f, :, WIDE:] for f in range(count)], axis=1)
        total += dot_nt(ends, tails)
        return (rhs[...] - total).astype(jnp.bfloat16)

    def apply(e):
        pltpu.make_async_copy(piv.at[e], pb.at[e], psem.at[e]).wait()
        scaled[...] = jnp.where(row == e, dot_nt(held[...], pb[e]), scaled[...])

    held[...] = residual(0)

    def step(e, carry):
        apply(e - 1)
        held[...] = residual(e)
        return carry

    lax.fori_loop(1, elems, step, 0)
    apply(elems - 1)
    own_out[...] = scaled[...]
    bucket = side_out.shape[0]
    for k in range(bucket):
        side_out[k : k + 1] = scaled[pl.ds(send[k], 1), :]
        across_out[k : k + 1] = scaled[pl.ds(send[bucket + k], 1), :]


def solve_kernel(last, table, back, side_m, own_m, across_m, side_s, own_s, across_s, *refs):
    outs = refs[:3] if last else refs[:1]
    mats, items, ahead, behind, sems = refs[len(outs) :]
    bucket = side_s.shape[0]
    elems = own_s.shape[0]
    width = own_s.shape[1]
    lines = table.shape[0] // LMAX
    tail = width - WIDE

    def load(p, r):
        slot = r * LMAX + p
        at = p * lines + r
        item = table[slot]
        sources = (
            (side_m, 0, bucket),
            (own_m, bucket, bucket + elems),
            (across_m, bucket + elems, 2 * bucket + elems),
        )
        for source, low, high in sources:

            @pl.when((item >= low) & (item < high))
            def _(source=source, low=low):
                pltpu.make_async_copy(source.at[item - low], mats.at[at], sems.at[at]).start()

    for p in range(LMAX):
        for r in range(lines):
            load(p, r)

    items[:bucket] = side_s[...]
    items[bucket : bucket + elems] = own_s[...]
    items[bucket + elems :] = across_s[...]
    sublanes = ahead.shape[1]
    row = lax.broadcasted_iota(jnp.int32, (sublanes, width), 0)

    def sweep_step(p, x, half):
        carried = jnp.zeros((sublanes, width), jnp.float32)
        for r in range(lines):
            at = p * lines + r
            lead = dot_nn(x, mats[at, :, half * WIDE : (half + 1) * WIDE])
            ending = dot_nn(x, mats[at, :, 2 * WIDE :])[:, half * tail : (half + 1) * tail]
            live = table[r * LMAX + p] >= 0
            carried = jnp.where((row == r) & live, jnp.concatenate([lead, ending], axis=1), carried)
        return carried

    for p in range(LMAX):
        ahead[p] = jnp.zeros((sublanes, width), jnp.float32)
        for r in range(lines):
            item = table[r * LMAX + p]

            @pl.when(item >= 0)
            def _(p=p, r=r, item=item):
                ahead[p, r : r + 1, :] = items[pl.ds(item, 1), :]

    x = None
    for p in range(LMAX):
        for r in range(lines):

            @pl.when(table[r * LMAX + p] >= 0)
            def _(p=p, r=r):
                at = p * lines + r
                pltpu.make_async_copy(own_m.at[0], mats.at[at], sems.at[at]).wait()

        value = ahead[p]
        if p > 0:
            value = value - sweep_step(p, x, 0)
            ahead[p] = value
        x = value.astype(jnp.bfloat16)
    x = None
    for p in reversed(range(LMAX)):
        value = ahead[p]
        if p < LMAX - 1:
            value = value - sweep_step(p, x, 1)
        behind[p] = value
        x = value.astype(jnp.bfloat16)
    if last:
        at = 0
        for out in outs:
            for k in range(out.shape[0]):
                slot = back[at + k]
                out[k : k + 1] = behind[slot % LMAX, pl.ds(slot // LMAX, 1), :]
            at += out.shape[0]
    else:
        (out,) = outs
        for p in range(LMAX):
            items[p * lines : (p + 1) * lines] = behind[p, :lines, :]
        out[...] = items[...].astype(jnp.bfloat16)


def place_kernel(index, side, own, across, out, items):
    bucket = side.shape[0]
    elems = own.shape[0]
    items[:bucket] = side[...]
    items[bucket : bucket + elems] = own[...]
    items[bucket + elems :] = across[...]
    for e in range(elems):
        out[e : e + 1] = items[pl.ds(index[e], 1), :]


def pack_order(selected, bucket):
    members = jnp.arange(selected.shape[0], dtype=jnp.int32)
    before = (members[None, :] <= members[:, None]) & selected[None, :]
    ordering = jnp.sum(before.astype(jnp.int32), axis=1) - 1
    positions = jnp.arange(bucket, dtype=jnp.int32)[:, None]
    matches = selected[None, :] & (ordering[None, :] == positions)
    picked = jnp.sum(jnp.where(matches, members[None, :], 0), axis=1)
    return (picked, jnp.any(matches, axis=1), jnp.clip(ordering, 0, bucket - 1))


def body(
    right_side,
    start_state,
    pivot_inverse,
    lower_block,
    upper_block,
    face_blocks,
    neighbours,
    element_slot,
):
    elems, width = right_side.shape
    faces = face_blocks.shape[1]
    bucket = elems // 2
    slot_count = 2 * elems
    lines = slot_count // LMAX
    packed = 2 * width
    devices = lax.axis_size("dom")
    me = lax.axis_index("dom").astype(jnp.int32)
    odd = me % 2 == 1
    side = jnp.where(odd, me - 1, me + 1)
    across = jnp.where(odd, me + 1, me - 1)
    side_pairs = [(i, i ^ 1) for i in range(devices)]
    across_pairs = [(i, i + 1) for i in range(1, devices - 1, 2)]
    across_pairs = across_pairs + [(j, i) for i, j in across_pairs]

    def to_side(array):
        return lax.ppermute(array, "dom", side_pairs)

    def to_across(array):
        return lax.ppermute(array, "dom", across_pairs)

    f32, bf16 = jnp.float32, jnp.bfloat16
    block = (width, width)
    pair = (width, packed)
    dma = pltpu.SemaphoreType.DMA

    rounded = start_state.astype(bf16)
    owner = element_slot // slot_count
    code = (element_slot - (me - 1) * slot_count).astype(bf16)
    column = lax.broadcasted_iota(jnp.int32, (elems, 128), 1)
    halo = jnp.concatenate([rounded, jnp.where(column == 0, code[:, None], jnp.zeros((), bf16))[:, : 384 - width]], axis=1)
    halo_across = to_across(halo)
    halo_side = to_side(halo)
    outgoing, side_pack = pl.pallas_call(
        functools.partial(outgoing_kernel, slot_count),
        out_shape=[jax.ShapeDtypeStruct((bucket,) + pair, bf16)] * 2,
        in_specs=[SMEM, SMEM, HBM, HBM, HBM],
        out_specs=[HBM, HBM],
        scratch_shapes=[pltpu.VMEM((2 * bucket,) + block, bf16)] * 3
        + [pltpu.VMEM((2 * bucket,) + pair, bf16), dma((3, 2 * bucket)), dma((2 * bucket,))],
        compiler_params=ROOMY,
        cost_estimate=SMALL,
        name="outgoing",
    )(element_slot, jnp.stack([across, side]), pivot_inverse, lower_block, upper_block)
    outgoing, side_pack, halo_across, halo_side, pivot_inverse, face_blocks = lax.optimization_barrier(
        (outgoing, side_pack, halo_across, halo_side, pivot_inverse, face_blocks)
    )
    across_in = to_across(outgoing)
    side_in = to_side(side_pack)
    state_side, state_across = halo_side[:, :width], halo_across[:, :width]
    slot_side = halo_side[:, width].astype(jnp.int32) + (side - 1) * slot_count
    slot_across = halo_across[:, width].astype(jnp.int32) + (across - 1) * slot_count

    own_pack = pl.pallas_call(
        functools.partial(staying_kernel, slot_count),
        out_shape=jax.ShapeDtypeStruct((elems,) + pair, bf16),
        in_specs=[SMEM, SMEM, HBM, HBM, HBM],
        out_specs=HBM,
        scratch_shapes=[pltpu.VMEM((elems,) + block, bf16)] * 3
        + [pltpu.VMEM((elems,) + pair, bf16), dma((3, elems)), dma((elems,))],
        compiler_params=ROOMY,
        cost_estimate=SMALL,
        name="staying",
    )(element_slot, me[None], pivot_inverse, lower_block, upper_block)

    side_index, _, side_rank = pack_order(owner == side, bucket)
    across_index, _, across_rank = pack_order(owner == across, bucket)
    send_index = jnp.concatenate([side_index, across_index])
    spread = jnp.arange(elems, dtype=jnp.int32)
    item_of_own = jnp.where(
        owner == me,
        bucket + spread,
        jnp.where(owner == side, side_rank, bucket + elems + across_rank),
    )
    across_live = (across >= 0) & (across < devices)
    in_side, in_side_valid, _ = pack_order(slot_side // slot_count == me, bucket)
    in_across, in_across_valid, _ = pack_order((slot_across // slot_count == me) & across_live, bucket)
    item_slot = jnp.concatenate(
        [
            jnp.where(in_side_valid, slot_side[in_side] % slot_count, -1),
            jnp.where(owner == me, element_slot % slot_count, -1),
            jnp.where(in_across_valid, slot_across[in_across] % slot_count, -1),
        ]
    )
    everything = jnp.arange(slot_count, dtype=jnp.int32)
    slot_matches = item_slot[None, :] == everything[:, None]
    table = jnp.max(jnp.where(slot_matches, everything[None, :], -1), axis=1)
    back = jnp.maximum(item_slot, 0)

    home = neighbours // elems
    within = neighbours % elems
    near = jnp.where(home == me, elems, jnp.where(home == side, 0, 2 * elems)) + within
    near = jnp.where(neighbours >= 0, near, -1)
    all_slots = jnp.concatenate([slot_side, element_slot, slot_across])
    place = all_slots[jnp.maximum(near, 0)]
    place_owner = place // slot_count
    place_slot = place % slot_count
    place_row = (place_slot % LMAX) * lines + place_slot // LMAX
    across_chip = across // 2
    far = jnp.where(
        place_owner == me,
        0,
        jnp.where(
            place_owner == side,
            slot_count,
            jnp.where(place_owner // 2 == across_chip, 2 * slot_count, 4 * slot_count)
            + (place_owner % 2) * slot_count,
        ),
    )
    far = jnp.where(neighbours >= 0, far + place_row, -1)

    def face_part(index, parts):
        counts = tuple(part.shape[0] for part in parts)
        return pl.pallas_call(
            functools.partial(face_kernel, counts),
            out_shape=[
                jax.ShapeDtypeStruct((bucket, width), f32),
                jax.ShapeDtypeStruct((bucket, width), f32),
                jax.ShapeDtypeStruct((elems, width), f32),
            ],
            in_specs=[SMEM, VMEM, VMEM] + [VMEM] * len(parts) + [HBM, HBM],
            out_specs=[VMEM] * 3,
            scratch_shapes=[
                pltpu.VMEM((sum(counts), width), bf16),
                pltpu.VMEM((faces * elems, width), bf16),
                pltpu.VMEM((elems, width), bf16),
                pltpu.VMEM((elems, width), f32),
                pltpu.VMEM((elems, faces) + block, bf16),
                pltpu.VMEM((elems,) + block, bf16),
                dma((elems,)),
                dma((elems,)),
            ],
            compiler_params=FACING,
            cost_estimate=SMALL,
            name="faces",
        )(send_index, index.reshape(-1, 1), right_side, *parts, face_blocks, pivot_inverse)

    def solve(last, side_s, own_s, across_s):
        if last:
            shapes = [(bucket, width), (elems, width), (bucket, width)]
            out_shape = [jax.ShapeDtypeStruct(shape, f32) for shape in shapes]
        else:
            out_shape = [jax.ShapeDtypeStruct((slot_count, width), bf16)]
        return pl.pallas_call(
            functools.partial(solve_kernel, last),
            out_shape=out_shape,
            in_specs=[SMEM, SMEM, HBM, HBM, HBM, VMEM, VMEM, VMEM],
            out_specs=[VMEM] * len(out_shape),
            scratch_shapes=[
                pltpu.VMEM((slot_count,) + pair, bf16),
                pltpu.VMEM((slot_count, width), f32),
                pltpu.VMEM((LMAX, 8, width), f32),
                pltpu.VMEM((LMAX, 8, width), f32),
                dma((slot_count,)),
            ],
            compiler_params=SNUG,
            cost_estimate=SMALL,
            name="solve",
        )(table, back, side_in, own_pack, across_in, side_s, own_s, across_s)

    index, parts = near, [state_side, rounded, state_across]
    for sweep in range(SWEEPS):
        scaled_side, scaled_across, scaled_own = face_part(index, parts)
        got_across = to_across(scaled_across)
        got_side = to_side(scaled_side)
        solved = solve(sweep == SWEEPS - 1, got_side, scaled_own, got_across)
        if sweep < SWEEPS - 1:
            (mine,) = solved
            beside = to_side(mine)
            chip = jnp.where(
                odd, jnp.concatenate([beside, mine]), jnp.concatenate([mine, beside])
            )
            over = to_across(chip)
            under = to_side(over)
            index, parts = far, [mine, beside, over, under]
    back_side, back_own, back_across = solved
    back_across = to_across(back_across)
    back_side = to_side(back_side)
    return pl.pallas_call(
        place_kernel,
        out_shape=jax.ShapeDtypeStruct((elems, width), f32),
        in_specs=[SMEM, VMEM, VMEM, VMEM],
        out_specs=VMEM,
        scratch_shapes=[pltpu.VMEM((slot_count, width), f32)],
        name="place",
    )(item_of_own, back_side, back_own, back_across)


def solution(mesh):
    placed = (
        P("dom", None),
        P("dom", None),
        P("dom", None, None),
        P("dom", None, None),
        P("dom", None, None),
        P("dom", None, None, None),
        P(None, "dom"),
        P("dom"),
    )
    return jax.shard_map(
        body, mesh=mesh, in_specs=placed, out_specs=P("dom", None), check_vma=False
    )
```

```python
import functools

import jax
import jax.numpy as jnp
from jax import lax
from jax.experimental import pallas as pl
from jax.experimental.pallas import tpu as pltpu
from jax.sharding import PartitionSpec as P

LMAX = 8
FIRST = 4
SIDES = 4
SWEEPS = 2
WIDE = 256
HBM = pl.BlockSpec(memory_space=pltpu.HBM)
SMEM = pl.BlockSpec(memory_space=pltpu.SMEM)
VMEM = pl.BlockSpec(memory_space=pltpu.VMEM)
ROOMY = pltpu.CompilerParams(vmem_limit_bytes=57 << 20)
FACING = pltpu.CompilerParams(vmem_limit_bytes=50 << 20)
SNUG = pltpu.CompilerParams(vmem_limit_bytes=52 << 20)
SMALL = pl.CostEstimate(flops=1 << 20, bytes_accessed=1 << 20, transcendentals=0)
NT = (((1,), (1,)), ((), ()))


def dot_nt(a, b):
    return lax.dot_general(a, b, NT, preferred_element_type=jnp.float32)


def dot_nn(a, b):
    return jnp.dot(a, b, preferred_element_type=jnp.float32)


def product(block, pivot):
    return dot_nt(block.T, pivot).astype(jnp.bfloat16)


def put(got, out, half):
    width = got.shape[1]
    tail = width - WIDE
    out[:, pl.ds(pl.multiple_of(half * WIDE, WIDE), WIDE)] = got[:, :WIDE]

    @pl.when(half == 0)
    def _():
        out[:, 2 * WIDE : 2 * WIDE + tail] = got[:, WIDE:]

    @pl.when(half == 1)
    def _():
        out[:, 2 * WIDE + tail :] = got[:, WIDE:]


def pair_product(pivot, lower, upper, out):
    both = jnp.concatenate([lower.T, upper.T], axis=0)
    got = dot_nt(both, pivot).astype(jnp.bfloat16)
    width = pivot.shape[0]
    out[:, :WIDE] = got[:width, :WIDE]
    out[:, WIDE : 2 * WIDE] = got[width:, :WIDE]
    out[:, 2 * WIDE :] = jnp.concatenate([got[:width, WIDE:], got[width:, WIDE:]], axis=1)


def places_taken(slots, owner, slot_count, taken):
    for e in range(slots.shape[0]):
        mine = slots[e] // slot_count == owner
        taken = jnp.where(mine, taken | (jnp.int32(1) << (slots[e] % slot_count)), taken)
    return taken


def is_taken(taken, slot):
    return ((taken >> slot) & 1) == 1


def block_jobs(slot, taken, hit, blind, seen, extra):
    jobs = []
    position = slot % LMAX
    for possible, beside in ((position > 0, slot - 1), (position < LMAX - 1, slot + 1)):
        possible = hit & possible
        early = possible & (seen < blind)
        late = possible & (seen >= blind) & is_taken(taken, jnp.clip(beside, 0, 31))
        jobs.append((early, late, seen, extra))
        seen = seen + possible.astype(jnp.int32)
        extra = extra + late.astype(jnp.int32)
    return jobs, seen, extra


def run_jobs(count, piv, pb, mb, stage, outs, insem, outsem):
    def pair_copies(at):
        return [pltpu.make_async_copy(stage.at[at], out, outsem.at[at]) for out in outs]

    def step(m, carry):
        pltpu.make_async_copy(piv.at[0], pb.at[m], insem.at[0, m]).wait()
        pltpu.make_async_copy(piv.at[0], mb.at[m], insem.at[1, m]).wait()
        put(product(mb[m], pb[m]), stage.at[m // 2], m % 2)
        for j, copy in enumerate(pair_copies(m // 2)):

            @pl.when((m // 2 == j) & ((m % 2 == 1) | (m == count - 1)))
            def _(copy=copy):
                copy.start()

        return carry

    lax.fori_loop(0, count, step, 0)
    for j in range(len(outs)):

        @pl.when(2 * j < count)
        def _(j=j):
            pltpu.make_async_copy(stage.at[j], outs[j], outsem.at[j]).wait()


def first_kernel(slot_count, slots, across, piv, low, upp, out, pb, mb, stage, insem, outsem):
    blind = 2 * out.shape[0]
    seen, extra = jnp.int32(0), jnp.int32(0)
    for e in range(slots.shape[0]):
        hit = slots[e] // slot_count == across[0]
        jobs, seen, extra = block_jobs(slots[e] % slot_count, jnp.int32(0), hit, blind, seen, extra)
        for (early, _, at, _), source in zip(jobs, (low, upp)):

            @pl.when(early)
            def _(e=e, at=at, source=source):
                pltpu.make_async_copy(piv.at[e], pb.at[at], insem.at[0, at]).start()
                pltpu.make_async_copy(source.at[e], mb.at[at], insem.at[1, at]).start()

    outs = [out.at[j] for j in range(out.shape[0])]
    run_jobs(jnp.minimum(seen, blind), piv, pb, mb, stage, outs, insem, outsem)


def rest_kernel(blind, sides, slot_count, slots, across_slots, far_slots, ids, piv, low, upp, *refs):
    side_outs, refs = refs[:sides], refs[sides:]
    outs = refs[: len(refs) - 11]
    share = side_outs[0].shape[0]
    pb, mb, stage, insem, outsem, sp, sl, su, side_stage, side_in, side_sem = refs[len(outs) :]
    across, side = ids[0], ids[1]
    taken = jnp.int32(0)
    for array in (slots, across_slots, far_slots):
        taken = places_taken(array, across, slot_count, taken)
    seen, extra, beside = jnp.int32(0), jnp.int32(0), jnp.int32(0)
    for e in range(slots.shape[0]):
        owner = slots[e] // slot_count
        jobs, seen, extra = block_jobs(slots[e] % slot_count, taken, owner == across, blind, seen, extra)
        for (_, late, _, at), source in zip(jobs, (low, upp)):

            @pl.when(late)
            def _(e=e, at=at, source=source):
                pltpu.make_async_copy(piv.at[e], pb.at[at], insem.at[0, at]).start()
                pltpu.make_async_copy(source.at[e], mb.at[at], insem.at[1, at]).start()

    for e in range(slots.shape[0]):
        hit = slots[e] // slot_count == side

        @pl.when(hit)
        def _(e=e, beside=beside):
            pltpu.make_async_copy(piv.at[e], sp.at[beside], side_in.at[0, beside]).start()
            pltpu.make_async_copy(low.at[e], sl.at[beside], side_in.at[1, beside]).start()
            pltpu.make_async_copy(upp.at[e], su.at[beside], side_in.at[2, beside]).start()

        beside = beside + hit.astype(jnp.int32)
    run_jobs(extra, piv, pb, mb, stage, outs, insem, outsem)

    def step(k, carry):
        pltpu.make_async_copy(piv.at[0], sp.at[k], side_in.at[0, k]).wait()
        pltpu.make_async_copy(piv.at[0], sl.at[k], side_in.at[1, k]).wait()
        pltpu.make_async_copy(piv.at[0], su.at[k], side_in.at[2, k]).wait()
        pair_product(sp[k], sl[k], su[k], side_stage.at[k])
        for j, side_out in enumerate(side_outs):

            @pl.when(k // share == j)
            def _(side_out=side_out):
                pltpu.make_async_copy(side_stage.at[k], side_out.at[k % share], side_sem.at[k]).start()

        return carry

    def drain(k, carry):
        pltpu.make_async_copy(side_stage.at[k], side_outs[0].at[0], side_sem.at[k]).wait()
        return carry

    lax.fori_loop(0, beside, step, 0)
    lax.fori_loop(0, beside, drain, 0)


def plan_kernel(blind, slot_count, slots, side_slots, across_slots, far_slots, ids, table, lower_at, upper_at, back, item_of_own, send, counts):
    across, side, me = ids[0], ids[1], ids[2]
    elems = slots.shape[0]
    bucket = elems // 2
    for k in range(slot_count):
        table[k] = jnp.int32(-1)
        lower_at[k] = jnp.int32(-1)
        upper_at[k] = jnp.int32(-1)
        back[k] = jnp.int32(0)
    for k in range(2 * bucket):
        send[k] = jnp.int32(0)
    taken, beyond = jnp.int32(0), jnp.int32(0)
    for array in (slots, side_slots, across_slots):
        taken = places_taken(array, me, slot_count, taken)
    for array in (slots, across_slots, far_slots):
        beyond = places_taken(array, across, slot_count, beyond)
    beside, over = jnp.int32(0), jnp.int32(0)
    seen, out_extra = jnp.int32(0), jnp.int32(0)
    for e in range(elems):
        owner, slot = slots[e] // slot_count, slots[e] % slot_count
        own, to_side, to_across = owner == me, owner == side, owner == across
        item_of_own[e] = jnp.where(own, bucket + e, jnp.where(to_side, beside, bucket + elems + over))

        @pl.when(own)
        def _(e=e, slot=slot):
            table[slot] = jnp.int32(bucket + e)
            lower_at[slot] = jnp.int32(2 * (bucket + e))
            upper_at[slot] = jnp.int32(2 * (bucket + e) + 1)
            back[bucket + e] = slot

        @pl.when(to_side)
        def _(e=e, beside=beside):
            send[beside] = jnp.int32(e)

        @pl.when(to_across)
        def _(e=e, over=over):
            send[bucket + over] = jnp.int32(e)

        _, seen, out_extra = block_jobs(slot, beyond, to_across, blind, seen, out_extra)
        beside = beside + to_side.astype(jnp.int32)
        over = over + to_across.astype(jnp.int32)
    k = jnp.int32(0)
    for e in range(elems):
        mine, slot = side_slots[e] // slot_count == me, side_slots[e] % slot_count

        @pl.when(mine)
        def _(k=k, slot=slot):
            table[slot] = k
            lower_at[slot] = 2 * k
            upper_at[slot] = 2 * k + 1
            back[k] = slot

        k = k + mine.astype(jnp.int32)
    k = jnp.int32(bucket + elems)
    seen, in_extra = jnp.int32(0), jnp.int32(0)
    for e in range(elems):
        mine, slot = across_slots[e] // slot_count == me, across_slots[e] % slot_count
        jobs, seen, in_extra = block_jobs(slot, taken, mine, blind, seen, in_extra)

        @pl.when(mine)
        def _(k=k, slot=slot, jobs=jobs):
            table[slot] = k
            back[k] = slot
            for (early, late, first, extra), at in zip(jobs, (lower_at, upper_at)):
                place = jnp.where(early, first, jnp.where(late, blind + extra, jnp.int32(-1)))
                at[slot] = jnp.where(place >= 0, place + 2 * (bucket + elems), place)

        k = k + mine.astype(jnp.int32)
    counts[0] = (out_extra + 1) // 2
    counts[1] = (in_extra + 1) // 2


def staying_kernel(slot_count, slots, me, piv, low, upp, own, pb, lb, ub, stage, insem, outsem):
    elems = slots.shape[0]

    def loads(e):
        return [
            pltpu.make_async_copy(src.at[e], dst.at[e], insem.at[i, e])
            for i, (src, dst) in enumerate(((piv, pb), (low, lb), (upp, ub)))
        ]

    def send(e):
        return pltpu.make_async_copy(stage.at[e], own.at[e], outsem.at[e])

    for e in range(elems):

        @pl.when(slots[e] // slot_count == me[0])
        def _(e=e):
            for copy in loads(e):
                copy.start()

    def step(e, carry):
        @pl.when(slots[e] // slot_count == me[0])
        def _():
            for copy in loads(e):
                copy.wait()
            pair_product(pb[e], lb[e], ub[e], stage.at[e])
            send(e).start()

        return carry

    lax.fori_loop(0, elems, step, 0)
    for e in range(elems):

        @pl.when(slots[e] // slot_count == me[0])
        def _(e=e):
            send(e).wait()


def face_kernel(counts, send, index, rhs, *refs):
    parts = refs[: len(counts)]
    faces, piv, side_out, across_out, own_out, rows, gathered, held, scaled, fb, pb, fsem, psem = refs[len(counts) :]
    elems, width = rhs.shape
    count = faces.shape[1]
    face_copies = [pltpu.make_async_copy(faces.at[e], fb.at[e], fsem.at[e]) for e in range(elems)]
    piv_copies = [pltpu.make_async_copy(piv.at[e], pb.at[e], psem.at[e]) for e in range(elems)]
    for face_copy, piv_copy in zip(face_copies, piv_copies):
        face_copy.start()
        piv_copy.start()
    at = 0
    for part, size in zip(parts, counts):
        rows[at : at + size] = part[...]
        at += size
    wanted = index[...] == lax.broadcasted_iota(jnp.int32, (count * elems, at), 1)
    picked = dot_nn(wanted.astype(jnp.bfloat16), rows[...]).astype(jnp.bfloat16)
    gathered[...] = picked
    ends = jnp.concatenate([picked[f * elems : (f + 1) * elems, WIDE:] for f in range(count)], axis=1)
    row = lax.broadcasted_iota(jnp.int32, (elems, width), 0)

    def residual(e):
        pltpu.make_async_copy(faces.at[e], fb.at[e], fsem.at[e]).wait()
        total = dot_nt(gathered[:elems, :WIDE], fb[e, 0, :, :WIDE])
        for f in range(1, count):
            total += dot_nt(gathered[f * elems : (f + 1) * elems, :WIDE], fb[e, f, :, :WIDE])
        tails = jnp.concatenate([fb[e, f, :, WIDE:] for f in range(count)], axis=1)
        total += dot_nt(ends, tails)
        return (rhs[...] - total).astype(jnp.bfloat16)

    def apply(e):
        pltpu.make_async_copy(piv.at[e], pb.at[e], psem.at[e]).wait()
        scaled[...] = jnp.where(row == e, dot_nt(held[...], pb[e]), scaled[...])

    held[...] = residual(0)

    def step(e, carry):
        apply(e - 1)
        held[...] = residual(e)
        return carry

    lax.fori_loop(1, elems, step, 0)
    apply(elems - 1)
    own_out[...] = scaled[...]
    bucket = side_out.shape[0]
    for k in range(bucket):
        side_out[k : k + 1] = scaled[pl.ds(send[k], 1), :]
        across_out[k : k + 1] = scaled[pl.ds(send[bucket + k], 1), :]


def solve_kernel(last, rests, table, lower_at, upper_at, back, counts, *refs):
    sides_m, (own_m, first_m), refs = refs[:SIDES], refs[SIDES : SIDES + 2], refs[SIDES + 2 :]
    rest_m = refs[:rests]
    side_s, own_s, across_s = refs[rests : rests + 3]
    refs = refs[rests + 3 :]
    outs = refs[:3] if last else refs[:1]
    mats, items, ahead, behind, sems, first_sem, rest_sem = refs[len(outs) :]
    bucket = side_s.shape[0]
    elems = own_s.shape[0]
    width = own_s.shape[1]
    lines = table.shape[0] // LMAX
    tail = width - WIDE
    firsts = first_m.shape[0]
    base = bucket + elems
    first_copy = pltpu.make_async_copy(first_m, mats.at[base : base + firsts], first_sem.at[0])
    first_copy.start()
    rest_copies = [
        pltpu.make_async_copy(rest, mats.at[base + firsts + j], rest_sem.at[j]) for j, rest in enumerate(rest_m)
    ]
    for j, copy in enumerate(rest_copies):

        @pl.when(j < counts[1])
        def _(copy=copy):
            copy.start()

    share = bucket // SIDES
    sources = [(side_m, j * share, (j + 1) * share) for j, side_m in enumerate(sides_m)] + [(own_m, bucket, base)]
    for p in range(LMAX):
        for r in range(lines):
            item = table[r * LMAX + p]
            for source, low, high in sources:

                @pl.when((item >= low) & (item < high))
                def _(source=source, low=low, item=item, p=p, r=r):
                    sem = sems.at[p * lines + r]
                    pltpu.make_async_copy(source.at[item - low], mats.at[item], sem).start()

    items[:bucket] = side_s[...]
    items[bucket : bucket + elems] = own_s[...]
    items[bucket + elems :] = across_s[...]
    sublanes = ahead.shape[1]
    row = lax.broadcasted_iota(jnp.int32, (sublanes, width), 0)

    def sweep_step(p, x, places):
        carried = jnp.zeros((sublanes, width), jnp.float32)
        for r in range(lines):
            place = places[r * LMAX + p]
            at = jnp.maximum(place, 0)
            unit, half = at // 2, at % 2
            lead = dot_nn(x, mats[unit, :, pl.ds(pl.multiple_of(half * WIDE, WIDE), WIDE)])
            ending = dot_nn(x, mats[unit, :, 2 * WIDE :])
            ending = jnp.where(half == 0, ending[:, :tail], ending[:, tail:])
            carried = jnp.where((row == r) & (place >= 0), jnp.concatenate([lead, ending], axis=1), carried)
        return carried

    for p in range(LMAX):
        ahead[p] = jnp.zeros((sublanes, width), jnp.float32)
        for r in range(lines):
            item = table[r * LMAX + p]

            @pl.when(item >= 0)
            def _(p=p, r=r, item=item):
                ahead[p, r : r + 1, :] = items[pl.ds(item, 1), :]

    x = None
    for p in range(LMAX):
        for r in range(lines):

            item = table[r * LMAX + p]

            @pl.when((item >= 0) & (item < base))
            def _(p=p, r=r, item=item):
                pltpu.make_async_copy(own_m.at[0], mats.at[item], sems.at[p * lines + r]).wait()

        if p == 1:
            first_copy.wait()
            for j, copy in enumerate(rest_copies):

                @pl.when(j < counts[1])
                def _(copy=copy):
                    copy.wait()

        value = ahead[p]
        if p > 0:
            value = value - sweep_step(p, x, lower_at)
            ahead[p] = value
        x = value.astype(jnp.bfloat16)
    x = None
    for p in reversed(range(LMAX)):
        value = ahead[p]
        if p < LMAX - 1:
            value = value - sweep_step(p, x, upper_at)
        behind[p] = value
        x = value.astype(jnp.bfloat16)
    if last:
        at = 0
        for out in outs:
            for k in range(out.shape[0]):
                slot = back[at + k]
                out[k : k + 1] = behind[slot % LMAX, pl.ds(slot // LMAX, 1), :]
            at += out.shape[0]
    else:
        (out,) = outs
        for p in range(LMAX):
            items[p * lines : (p + 1) * lines] = behind[p, :lines, :]
        out[...] = items[...].astype(jnp.bfloat16)


def place_kernel(index, side, own, across, out, items):
    bucket = side.shape[0]
    elems = own.shape[0]
    items[:bucket] = side[...]
    items[bucket : bucket + elems] = own[...]
    items[bucket + elems :] = across[...]
    for e in range(elems):
        out[e : e + 1] = items[pl.ds(index[e], 1), :]


def body(
    right_side,
    start_state,
    pivot_inverse,
    lower_block,
    upper_block,
    face_blocks,
    neighbours,
    element_slot,
):
    elems, width = right_side.shape
    faces = face_blocks.shape[1]
    bucket = elems // 2
    slot_count = 2 * elems
    lines = slot_count // LMAX
    packed = 2 * width
    devices = lax.axis_size("dom")
    me = lax.axis_index("dom").astype(jnp.int32)
    odd = me % 2 == 1
    side = jnp.where(odd, me - 1, me + 1)
    across = jnp.where(odd, me + 1, me - 1)
    side_pairs = [(i, i ^ 1) for i in range(devices)]
    up_pairs = [(i, i + 1) for i in range(1, devices - 1, 2)]
    down_pairs = [(j, i) for i, j in up_pairs]
    across_pairs = up_pairs + down_pairs

    def to_side(array):
        return lax.ppermute(array, "dom", side_pairs)

    def to_across(array):
        return lax.ppermute(array, "dom", across_pairs)

    f32, bf16 = jnp.float32, jnp.bfloat16
    block = (width, width)
    pair = (width, packed)
    dma = pltpu.SemaphoreType.DMA

    firsts, rests = FIRST, bucket - FIRST
    blind = 2 * firsts
    ids = jnp.stack([across, side, me])
    rounded = start_state.astype(bf16)
    code = (element_slot - (me - 1) * slot_count).astype(bf16)
    room = -width % 128
    column = lax.broadcasted_iota(jnp.int32, (elems, room), 1)

    def framed(first_code, second_code):
        extra = jnp.where(column == 0, first_code[:, None], second_code[:, None])
        return jnp.concatenate([rounded, extra], axis=1)

    halo_side = to_side(framed(code, code))
    halo_across = to_across(framed(code, halo_side[:, width]))
    across_live = (across >= 0) & (across < devices)
    nowhere = devices * slot_count
    across_mate = across ^ 1

    def slots_of(codes, home, live):
        return jnp.where(live, codes.astype(jnp.int32) + (home - 1) * slot_count, nowhere)

    first = pl.pallas_call(
        functools.partial(first_kernel, slot_count),
        out_shape=jax.ShapeDtypeStruct((firsts,) + pair, bf16),
        in_specs=[SMEM, SMEM, HBM, HBM, HBM],
        out_specs=HBM,
        scratch_shapes=[pltpu.VMEM((blind,) + block, bf16)] * 2
        + [pltpu.VMEM((firsts,) + pair, bf16), dma((2, blind)), dma((firsts,))],
        compiler_params=ROOMY,
        cost_estimate=SMALL,
        name="first",
    )(element_slot, across[None], pivot_inverse, lower_block, upper_block)
    first, halo_across, halo_side, pivot_inverse, face_blocks = lax.optimization_barrier(
        (first, halo_across, halo_side, pivot_inverse, face_blocks)
    )
    first_in = to_across(first)
    state_side, state_across = halo_side[:, :width], halo_across[:, :width]
    slot_side = slots_of(halo_side[:, width], side, True)
    slot_across = slots_of(halo_across[:, width], across, across_live)
    slot_far = slots_of(halo_across[:, width + 1], across_mate, across_live)
    made = pl.pallas_call(
        functools.partial(rest_kernel, blind, SIDES, slot_count),
        out_shape=[jax.ShapeDtypeStruct((bucket // SIDES,) + pair, bf16)] * SIDES
        + [jax.ShapeDtypeStruct(pair, bf16)] * rests,
        in_specs=[SMEM] * 4 + [HBM] * 3,
        out_specs=[HBM] * (SIDES + rests),
        scratch_shapes=[pltpu.VMEM((2 * rests,) + block, bf16)] * 2
        + [pltpu.VMEM((rests,) + pair, bf16), dma((2, 2 * rests)), dma((rests,))]
        + [pltpu.VMEM((bucket,) + block, bf16)] * 3
        + [pltpu.VMEM((bucket,) + pair, bf16), dma((3, bucket)), dma((bucket,))],
        compiler_params=ROOMY,
        cost_estimate=SMALL,
        name="rest",
    )(element_slot, slot_across, slot_far, ids, pivot_inverse, lower_block, upper_block)
    rest = made[SIDES:]
    side_in = tuple(to_side(part) for part in made[:SIDES])
    whole = jax.ShapeDtypeStruct((slot_count,), jnp.int32)
    some = jax.ShapeDtypeStruct((elems,), jnp.int32)
    table, lower_at, upper_at, back, item_of_own, send_index, counts = pl.pallas_call(
        functools.partial(plan_kernel, blind, slot_count),
        out_shape=[whole] * 4 + [some] * 2 + [jax.ShapeDtypeStruct((2,), jnp.int32)],
        in_specs=[SMEM] * 5,
        out_specs=[SMEM] * 7,
        cost_estimate=SMALL,
        name="plan",
    )(element_slot, slot_side, slot_across, slot_far, ids)

    own_pack = pl.pallas_call(
        functools.partial(staying_kernel, slot_count),
        out_shape=jax.ShapeDtypeStruct((elems,) + pair, bf16),
        in_specs=[SMEM, SMEM, HBM, HBM, HBM],
        out_specs=HBM,
        scratch_shapes=[pltpu.VMEM((elems,) + block, bf16)] * 3
        + [pltpu.VMEM((elems,) + pair, bf16), dma((3, elems)), dma((elems,))],
        compiler_params=ROOMY,
        cost_estimate=SMALL,
        name="staying",
    )(element_slot, me[None], pivot_inverse, lower_block, upper_block)

    home = neighbours // elems
    within = neighbours % elems
    near = jnp.where(home == me, elems, jnp.where(home == side, 0, 2 * elems)) + within
    near = jnp.where(neighbours >= 0, near, -1)
    all_slots = jnp.concatenate([slot_side, element_slot, slot_across])
    place = all_slots[jnp.maximum(near, 0)]
    place_owner = place // slot_count
    place_slot = place % slot_count
    place_row = (place_slot % LMAX) * lines + place_slot // LMAX
    across_chip = across // 2
    far = jnp.where(
        place_owner == me,
        0,
        jnp.where(
            place_owner == side,
            slot_count,
            jnp.where(place_owner // 2 == across_chip, 2 * slot_count, 4 * slot_count)
            + (place_owner % 2) * slot_count,
        ),
    )
    far = jnp.where(neighbours >= 0, far + place_row, -1)

    def face_part(index, parts):
        counts = tuple(part.shape[0] for part in parts)
        return pl.pallas_call(
            functools.partial(face_kernel, counts),
            out_shape=[
                jax.ShapeDtypeStruct((bucket, width), f32),
                jax.ShapeDtypeStruct((bucket, width), f32),
                jax.ShapeDtypeStruct((elems, width), f32),
            ],
            in_specs=[SMEM, VMEM, VMEM] + [VMEM] * len(parts) + [HBM, HBM],
            out_specs=[VMEM] * 3,
            scratch_shapes=[
                pltpu.VMEM((sum(counts), width), bf16),
                pltpu.VMEM((faces * elems, width), bf16),
                pltpu.VMEM((elems, width), bf16),
                pltpu.VMEM((elems, width), f32),
                pltpu.VMEM((elems, faces) + block, bf16),
                pltpu.VMEM((elems,) + block, bf16),
                dma((elems,)),
                dma((elems,)),
            ],
            compiler_params=FACING,
            cost_estimate=SMALL,
            name="faces",
        )(send_index, index.reshape(-1, 1), right_side, *parts, face_blocks, pivot_inverse)

    def solve(last, blocks, side_s, own_s, across_s):
        if last:
            shapes = [(bucket, width), (elems, width), (bucket, width)]
            out_shape = [jax.ShapeDtypeStruct(shape, f32) for shape in shapes]
        else:
            out_shape = [jax.ShapeDtypeStruct((slot_count, width), bf16)]
        return pl.pallas_call(
            functools.partial(solve_kernel, last, rests),
            out_shape=out_shape,
            in_specs=[SMEM] * 5 + [HBM] * (SIDES + 2 + rests) + [VMEM] * 3,
            out_specs=[VMEM] * len(out_shape),
            scratch_shapes=[
                pltpu.VMEM((slot_count,) + pair, bf16),
                pltpu.VMEM((slot_count, width), f32),
                pltpu.VMEM((LMAX, 8, width), f32),
                pltpu.VMEM((LMAX, 8, width), f32),
                dma((slot_count,)),
                dma((1,)),
                dma((rests,)),
            ],
            compiler_params=SNUG,
            cost_estimate=SMALL,
            name="solve",
        )(table, lower_at, upper_at, back, counts, *blocks, side_s, own_s, across_s)

    def exchange(going, coming, *arrays):
        *blocks, vectors = arrays
        got = []
        for j, block in enumerate(blocks):
            pairs = (up_pairs if j < going else []) + (down_pairs if j < coming else [])
            got.append(lax.ppermute(block, "dom", pairs) if pairs else jnp.zeros_like(block))
        return (*got, to_across(vectors))

    exchanges = [
        functools.partial(exchange, going, coming) for going in range(rests + 1) for coming in range(rests + 1)
    ]
    index, parts = near, [state_side, rounded, state_across]
    for sweep in range(SWEEPS):
        scaled_side, scaled_across, scaled_own = face_part(index, parts)
        got_side = to_side(scaled_side)
        if sweep == 0:
            rest, scaled_across, counts, own_pack, first_in, side_in, got_side = lax.optimization_barrier(
                (tuple(rest), scaled_across, counts, own_pack, first_in, side_in, got_side)
            )
            going = jnp.where(odd, counts[0], counts[1])
            coming = jnp.where(odd, counts[1], counts[0])
            branch = going * (rests + 1) + coming
            *rest_in, got_across = lax.switch(branch, exchanges, *rest, scaled_across)
        else:
            got_across = to_across(scaled_across)
        blocks = (*side_in, own_pack, first_in, *rest_in)
        solved = solve(sweep == SWEEPS - 1, blocks, got_side, scaled_own, got_across)
        if sweep < SWEEPS - 1:
            (mine,) = solved
            beside = to_side(mine)
            chip = jnp.where(
                odd, jnp.concatenate([beside, mine]), jnp.concatenate([mine, beside])
            )
            over = to_across(chip)
            under = to_side(over)
            index, parts = far, [mine, beside, over, under]
    back_side, back_own, back_across = solved
    back_across = to_across(back_across)
    back_side = to_side(back_side)
    return pl.pallas_call(
        place_kernel,
        out_shape=jax.ShapeDtypeStruct((elems, width), f32),
        in_specs=[SMEM, VMEM, VMEM, VMEM],
        out_specs=VMEM,
        scratch_shapes=[pltpu.VMEM((slot_count, width), f32)],
        name="place",
    )(item_of_own, back_side, back_own, back_across)


def solution(mesh):
    placed = (
        P("dom", None),
        P("dom", None),
        P("dom", None, None),
        P("dom", None, None),
        P("dom", None, None),
        P("dom", None, None, None),
        P(None, "dom"),
        P("dom"),
    )
    return jax.shard_map(
        body, mesh=mesh, in_specs=placed, out_specs=P("dom", None), check_vma=False
    )
```

```python
import functools

import jax
import jax.numpy as jnp
from jax import lax
from jax.experimental import pallas as pl
from jax.experimental.pallas import tpu as pltpu
from jax.sharding import PartitionSpec as P

LMAX = 8
FIRST = 4
SIDES = 4
SWEEPS = 2
WIDE = 256
HBM = pl.BlockSpec(memory_space=pltpu.HBM)
SMEM = pl.BlockSpec(memory_space=pltpu.SMEM)
VMEM = pl.BlockSpec(memory_space=pltpu.VMEM)
ROOMY = pltpu.CompilerParams(vmem_limit_bytes=57 << 20)
FACING = pltpu.CompilerParams(vmem_limit_bytes=50 << 20)
SNUG = pltpu.CompilerParams(vmem_limit_bytes=52 << 20)
SMALL = pl.CostEstimate(flops=1 << 20, bytes_accessed=1 << 20, transcendentals=0)
NT = (((1,), (1,)), ((), ()))


def dot_nt(a, b):
    return lax.dot_general(a, b, NT, preferred_element_type=jnp.float32)


def dot_nn(a, b):
    return jnp.dot(a, b, preferred_element_type=jnp.float32)


def product(block, pivot):
    return dot_nt(block.T, pivot).astype(jnp.bfloat16)


def put(got, out, half):
    width = got.shape[1]
    tail = width - WIDE
    out[:, pl.ds(pl.multiple_of(half * WIDE, WIDE), WIDE)] = got[:, :WIDE]

    @pl.when(half == 0)
    def _():
        out[:, 2 * WIDE : 2 * WIDE + tail] = got[:, WIDE:]

    @pl.when(half == 1)
    def _():
        out[:, 2 * WIDE + tail :] = got[:, WIDE:]


def pair_product(pivot, lower, upper, out):
    both = jnp.concatenate([lower.T, upper.T], axis=0)
    got = dot_nt(both, pivot).astype(jnp.bfloat16)
    width = pivot.shape[0]
    out[:, :WIDE] = got[:width, :WIDE]
    out[:, WIDE : 2 * WIDE] = got[width:, :WIDE]
    out[:, 2 * WIDE :] = jnp.concatenate([got[:width, WIDE:], got[width:, WIDE:]], axis=1)


def places_taken(slots, owner, slot_count, taken):
    for e in range(slots.shape[0]):
        mine = slots[e] // slot_count == owner
        taken = jnp.where(mine, taken | (jnp.int32(1) << (slots[e] % slot_count)), taken)
    return taken


def is_taken(taken, slot):
    return ((taken >> slot) & 1) == 1


def block_jobs(slot, taken, hit, blind, seen, extra):
    jobs = []
    position = slot % LMAX
    for possible, beside in ((position > 0, slot - 1), (position < LMAX - 1, slot + 1)):
        possible = hit & possible
        early = possible & (seen < blind)
        late = possible & (seen >= blind) & is_taken(taken, jnp.clip(beside, 0, 31))
        jobs.append((early, late, seen, extra))
        seen = seen + possible.astype(jnp.int32)
        extra = extra + late.astype(jnp.int32)
    return jobs, seen, extra


def run_jobs(count, piv, pb, mb, stage, outs, insem, outsem):
    def pair_copies(at):
        return [pltpu.make_async_copy(stage.at[at], out, outsem.at[at]) for out in outs]

    def step(m, carry):
        pltpu.make_async_copy(piv.at[0], pb.at[m], insem.at[0, m]).wait()
        pltpu.make_async_copy(piv.at[0], mb.at[m], insem.at[1, m]).wait()
        put(product(mb[m], pb[m]), stage.at[m // 2], m % 2)
        for j, copy in enumerate(pair_copies(m // 2)):

            @pl.when((m // 2 == j) & ((m % 2 == 1) | (m == count - 1)))
            def _(copy=copy):
                copy.start()

        return carry

    lax.fori_loop(0, count, step, 0)
    for j in range(len(outs)):

        @pl.when(2 * j < count)
        def _(j=j):
            pltpu.make_async_copy(stage.at[j], outs[j], outsem.at[j]).wait()


def first_kernel(slot_count, slots, across, piv, low, upp, out, pb, mb, stage, insem, outsem):
    blind = 2 * out.shape[0]
    seen, extra = jnp.int32(0), jnp.int32(0)
    for e in range(slots.shape[0]):
        hit = slots[e] // slot_count == across[0]
        jobs, seen, extra = block_jobs(slots[e] % slot_count, jnp.int32(0), hit, blind, seen, extra)
        for (early, _, at, _), source in zip(jobs, (low, upp)):

            @pl.when(early)
            def _(e=e, at=at, source=source):
                pltpu.make_async_copy(piv.at[e], pb.at[at], insem.at[0, at]).start()
                pltpu.make_async_copy(source.at[e], mb.at[at], insem.at[1, at]).start()

    outs = [out.at[j] for j in range(out.shape[0])]
    run_jobs(jnp.minimum(seen, blind), piv, pb, mb, stage, outs, insem, outsem)


def rest_kernel(blind, sides, slot_count, slots, across_slots, far_slots, ids, piv, low, upp, *refs):
    side_outs, refs = refs[:sides], refs[sides:]
    outs = refs[: len(refs) - 11]
    share = side_outs[0].shape[0]
    pb, mb, stage, insem, outsem, sp, sl, su, side_stage, side_in, side_sem = refs[len(outs) :]
    across, side = ids[0], ids[1]
    taken = jnp.int32(0)
    for array in (slots, across_slots, far_slots):
        taken = places_taken(array, across, slot_count, taken)
    seen, extra, beside = jnp.int32(0), jnp.int32(0), jnp.int32(0)
    for e in range(slots.shape[0]):
        owner = slots[e] // slot_count
        jobs, seen, extra = block_jobs(slots[e] % slot_count, taken, owner == across, blind, seen, extra)
        for (_, late, _, at), source in zip(jobs, (low, upp)):

            @pl.when(late)
            def _(e=e, at=at, source=source):
                pltpu.make_async_copy(piv.at[e], pb.at[at], insem.at[0, at]).start()
                pltpu.make_async_copy(source.at[e], mb.at[at], insem.at[1, at]).start()

    for e in range(slots.shape[0]):
        hit = slots[e] // slot_count == side

        @pl.when(hit)
        def _(e=e, beside=beside):
            pltpu.make_async_copy(piv.at[e], sp.at[beside], side_in.at[0, beside]).start()
            pltpu.make_async_copy(low.at[e], sl.at[beside], side_in.at[1, beside]).start()
            pltpu.make_async_copy(upp.at[e], su.at[beside], side_in.at[2, beside]).start()

        beside = beside + hit.astype(jnp.int32)
    run_jobs(extra, piv, pb, mb, stage, outs, insem, outsem)

    def step(k, carry):
        pltpu.make_async_copy(piv.at[0], sp.at[k], side_in.at[0, k]).wait()
        pltpu.make_async_copy(piv.at[0], sl.at[k], side_in.at[1, k]).wait()
        pltpu.make_async_copy(piv.at[0], su.at[k], side_in.at[2, k]).wait()
        pair_product(sp[k], sl[k], su[k], side_stage.at[k])
        for j, side_out in enumerate(side_outs):

            @pl.when(k // share == j)
            def _(side_out=side_out):
                pltpu.make_async_copy(side_stage.at[k], side_out.at[k % share], side_sem.at[k]).start()

        return carry

    def drain(k, carry):
        pltpu.make_async_copy(side_stage.at[k], side_outs[0].at[0], side_sem.at[k]).wait()
        return carry

    lax.fori_loop(0, beside, step, 0)
    lax.fori_loop(0, beside, drain, 0)


def plan_kernel(blind, slot_count, slots, side_slots, across_slots, far_slots, ids, table, lower_at, upper_at, back, item_of_own, send, counts):
    across, side, me = ids[0], ids[1], ids[2]
    elems = slots.shape[0]
    bucket = elems // 2
    for k in range(slot_count):
        table[k] = jnp.int32(-1)
        lower_at[k] = jnp.int32(-1)
        upper_at[k] = jnp.int32(-1)
        back[k] = jnp.int32(0)
    for k in range(2 * bucket):
        send[k] = jnp.int32(0)
    taken, beyond = jnp.int32(0), jnp.int32(0)
    for array in (slots, side_slots, across_slots):
        taken = places_taken(array, me, slot_count, taken)
    for array in (slots, across_slots, far_slots):
        beyond = places_taken(array, across, slot_count, beyond)
    beside, over = jnp.int32(0), jnp.int32(0)
    seen, out_extra = jnp.int32(0), jnp.int32(0)
    for e in range(elems):
        owner, slot = slots[e] // slot_count, slots[e] % slot_count
        own, to_side, to_across = owner == me, owner == side, owner == across
        item_of_own[e] = jnp.where(own, bucket + e, jnp.where(to_side, beside, bucket + elems + over))

        @pl.when(own)
        def _(e=e, slot=slot):
            table[slot] = jnp.int32(bucket + e)
            lower_at[slot] = jnp.int32(2 * (bucket + e))
            upper_at[slot] = jnp.int32(2 * (bucket + e) + 1)
            back[bucket + e] = slot

        @pl.when(to_side)
        def _(e=e, beside=beside):
            send[beside] = jnp.int32(e)

        @pl.when(to_across)
        def _(e=e, over=over):
            send[bucket + over] = jnp.int32(e)

        _, seen, out_extra = block_jobs(slot, beyond, to_across, blind, seen, out_extra)
        beside = beside + to_side.astype(jnp.int32)
        over = over + to_across.astype(jnp.int32)
    k = jnp.int32(0)
    for e in range(elems):
        mine, slot = side_slots[e] // slot_count == me, side_slots[e] % slot_count

        @pl.when(mine)
        def _(k=k, slot=slot):
            table[slot] = k
            lower_at[slot] = 2 * k
            upper_at[slot] = 2 * k + 1
            back[k] = slot

        k = k + mine.astype(jnp.int32)
    k = jnp.int32(bucket + elems)
    seen, in_extra = jnp.int32(0), jnp.int32(0)
    for e in range(elems):
        mine, slot = across_slots[e] // slot_count == me, across_slots[e] % slot_count
        jobs, seen, in_extra = block_jobs(slot, taken, mine, blind, seen, in_extra)

        @pl.when(mine)
        def _(k=k, slot=slot, jobs=jobs):
            table[slot] = k
            back[k] = slot
            for (early, late, first, extra), at in zip(jobs, (lower_at, upper_at)):
                place = jnp.where(early, first, jnp.where(late, blind + extra, jnp.int32(-1)))
                at[slot] = jnp.where(place >= 0, place + 2 * (bucket + elems), place)

        k = k + mine.astype(jnp.int32)
    counts[0] = (out_extra + 1) // 2
    counts[1] = (in_extra + 1) // 2


def staying_kernel(slot_count, slots, me, piv, low, upp, own, pb, lb, ub, stage, insem, outsem):
    elems = slots.shape[0]

    def loads(e):
        return [
            pltpu.make_async_copy(src.at[e], dst.at[e], insem.at[i, e])
            for i, (src, dst) in enumerate(((piv, pb), (low, lb), (upp, ub)))
        ]

    def send(e):
        return pltpu.make_async_copy(stage.at[e], own.at[e], outsem.at[e])

    for e in range(elems):

        @pl.when(slots[e] // slot_count == me[0])
        def _(e=e):
            for copy in loads(e):
                copy.start()

    def step(e, carry):
        @pl.when(slots[e] // slot_count == me[0])
        def _():
            for copy in loads(e):
                copy.wait()
            pair_product(pb[e], lb[e], ub[e], stage.at[e])
            send(e).start()

        return carry

    lax.fori_loop(0, elems, step, 0)
    for e in range(elems):

        @pl.when(slots[e] // slot_count == me[0])
        def _(e=e):
            send(e).wait()


def face_kernel(counts, send, index, rhs, *refs):
    parts = refs[: len(counts)]
    faces, piv, side_out, across_out, own_out, rows, gathered, flat, rhs_t, held, scaled, fb, pb, fsem, psem = refs[
        len(counts) :
    ]
    elems, width = rhs.shape
    count = faces.shape[1]
    for e in range(elems):
        pltpu.make_async_copy(faces.at[e], fb.at[e], fsem.at[e]).start()
        pltpu.make_async_copy(piv.at[e], pb.at[e], psem.at[e]).start()
    at = 0
    for part, size in zip(parts, counts):
        rows[at : at + size] = part[...]
        at += size
    wanted = index[...] == lax.broadcasted_iota(jnp.int32, (count * elems, at), 1)
    gathered[...] = dot_nn(wanted.astype(jnp.bfloat16), rows[...])
    flat[...] = jnp.zeros(flat.shape, jnp.float32)
    flat[:elems, :width] = rhs[...]
    rhs_t[...] = flat[...].T
    lanes = rhs_t.shape[1]
    column = lax.broadcasted_iota(jnp.int32, (width, lanes), 1)

    def residual(e):
        pltpu.make_async_copy(faces.at[e], fb.at[e], fsem.at[e]).wait()
        states = [gathered[pl.ds(f * elems + e, 1), :] for f in range(count)]

        def term(f, low, high):
            return fb[e, f, :, low:high].astype(jnp.float32) * states[f][:, low:high]

        lead, ending = None, None
        for f in range(count):
            for low in range(0, WIDE, lanes):
                more = term(f, low, low + lanes)
                lead = more if lead is None else lead + more
            more = term(f, WIDE, width)
            ending = more if ending is None else ending + more
        total = jnp.sum(lead, axis=1, keepdims=True) + jnp.sum(ending, axis=1, keepdims=True)
        return (rhs_t[:width] - total).astype(jnp.bfloat16)

    def apply(e):
        pltpu.make_async_copy(piv.at[e], pb.at[e], psem.at[e]).wait()
        scaled[:width] = jnp.where(column == e, dot_nn(pb[e], held[...]), scaled[:width])

    scaled[...] = jnp.zeros(scaled.shape, jnp.float32)
    held[...] = residual(0)

    def step(e, carry):
        apply(e - 1)
        held[...] = residual(e)
        return carry

    lax.fori_loop(1, elems, step, 0)
    apply(elems - 1)
    flat[...] = scaled[...].T
    own_out[...] = flat[:elems, :width]
    bucket = side_out.shape[0]
    for k in range(bucket):
        side_out[k : k + 1] = flat[pl.ds(send[k], 1), :][:, :width]
        across_out[k : k + 1] = flat[pl.ds(send[bucket + k], 1), :][:, :width]


def solve_kernel(last, rests, table, lower_at, upper_at, back, counts, *refs):
    sides_m, (own_m, first_m), refs = refs[:SIDES], refs[SIDES : SIDES + 2], refs[SIDES + 2 :]
    rest_m = refs[:rests]
    side_s, own_s, across_s = refs[rests : rests + 3]
    refs = refs[rests + 3 :]
    outs = refs[:3] if last else refs[:1]
    mats, items, ahead, behind, sems, first_sem, rest_sem = refs[len(outs) :]
    bucket = side_s.shape[0]
    elems = own_s.shape[0]
    width = own_s.shape[1]
    lines = table.shape[0] // LMAX
    tail = width - WIDE
    firsts = first_m.shape[0]
    base = bucket + elems
    first_copy = pltpu.make_async_copy(first_m, mats.at[base : base + firsts], first_sem.at[0])
    first_copy.start()
    rest_copies = [
        pltpu.make_async_copy(rest, mats.at[base + firsts + j], rest_sem.at[j]) for j, rest in enumerate(rest_m)
    ]
    for j, copy in enumerate(rest_copies):

        @pl.when(j < counts[1])
        def _(copy=copy):
            copy.start()

    share = bucket // SIDES
    sources = [(side_m, j * share, (j + 1) * share) for j, side_m in enumerate(sides_m)] + [(own_m, bucket, base)]
    for p in range(LMAX):
        for r in range(lines):
            item = table[r * LMAX + p]
            for source, low, high in sources:

                @pl.when((item >= low) & (item < high))
                def _(source=source, low=low, item=item, p=p, r=r):
                    sem = sems.at[p * lines + r]
                    pltpu.make_async_copy(source.at[item - low], mats.at[item], sem).start()

    items[:bucket] = side_s[...]
    items[bucket : bucket + elems] = own_s[...]
    items[bucket + elems :] = across_s[...]
    sublanes = ahead.shape[1]
    row = lax.broadcasted_iota(jnp.int32, (sublanes, width), 0)

    def sweep_step(p, x, places):
        carried = jnp.zeros((sublanes, width), jnp.float32)
        for r in range(lines):
            place = places[r * LMAX + p]
            at = jnp.maximum(place, 0)
            unit, half = at // 2, at % 2
            lead = dot_nn(x, mats[unit, :, pl.ds(pl.multiple_of(half * WIDE, WIDE), WIDE)])
            ending = dot_nn(x, mats[unit, :, 2 * WIDE :])
            ending = jnp.where(half == 0, ending[:, :tail], ending[:, tail:])
            carried = jnp.where((row == r) & (place >= 0), jnp.concatenate([lead, ending], axis=1), carried)
        return carried

    for p in range(LMAX):
        ahead[p] = jnp.zeros((sublanes, width), jnp.float32)
        for r in range(lines):
            item = table[r * LMAX + p]

            @pl.when(item >= 0)
            def _(p=p, r=r, item=item):
                ahead[p, r : r + 1, :] = items[pl.ds(item, 1), :]

    x = None
    for p in range(LMAX):
        for r in range(lines):

            item = table[r * LMAX + p]

            @pl.when((item >= 0) & (item < base))
            def _(p=p, r=r, item=item):
                pltpu.make_async_copy(own_m.at[0], mats.at[item], sems.at[p * lines + r]).wait()

        if p == 1:
            first_copy.wait()
            for j, copy in enumerate(rest_copies):

                @pl.when(j < counts[1])
                def _(copy=copy):
                    copy.wait()

        value = ahead[p]
        if p > 0:
            value = value - sweep_step(p, x, lower_at)
            ahead[p] = value
        x = value.astype(jnp.bfloat16)
    x = None
    for p in reversed(range(LMAX)):
        value = ahead[p]
        if p < LMAX - 1:
            value = value - sweep_step(p, x, upper_at)
        behind[p] = value
        x = value.astype(jnp.bfloat16)
    if last:
        at = 0
        for out in outs:
            for k in range(out.shape[0]):
                slot = back[at + k]
                out[k : k + 1] = behind[slot % LMAX, pl.ds(slot // LMAX, 1), :]
            at += out.shape[0]
    else:
        (out,) = outs
        for p in range(LMAX):
            items[p * lines : (p + 1) * lines] = behind[p, :lines, :]
        out[...] = items[...].astype(jnp.bfloat16)


def nothing_kernel(*outs):
    pass


def place_kernel(index, side, own, across, out, items):
    bucket = side.shape[0]
    elems = own.shape[0]
    items[:bucket] = side[...]
    items[bucket : bucket + elems] = own[...]
    items[bucket + elems :] = across[...]
    for e in range(elems):
        out[e : e + 1] = items[pl.ds(index[e], 1), :]


def body(
    right_side,
    start_state,
    pivot_inverse,
    lower_block,
    upper_block,
    face_blocks,
    neighbours,
    element_slot,
):
    elems, width = right_side.shape
    faces = face_blocks.shape[1]
    bucket = elems // 2
    slot_count = 2 * elems
    lines = slot_count // LMAX
    packed = 2 * width
    devices = lax.axis_size("dom")
    me = lax.axis_index("dom").astype(jnp.int32)
    odd = me % 2 == 1
    side = jnp.where(odd, me - 1, me + 1)
    across = jnp.where(odd, me + 1, me - 1)
    side_pairs = [(i, i ^ 1) for i in range(devices)]
    up_pairs = [(i, i + 1) for i in range(1, devices - 1, 2)]
    down_pairs = [(j, i) for i, j in up_pairs]
    across_pairs = up_pairs + down_pairs

    def to_side(array):
        return lax.ppermute(array, "dom", side_pairs)

    def to_across(array):
        return lax.ppermute(array, "dom", across_pairs)

    f32, bf16 = jnp.float32, jnp.bfloat16
    block = (width, width)
    pair = (width, packed)
    dma = pltpu.SemaphoreType.DMA

    firsts, rests = FIRST, bucket - FIRST
    blind = 2 * firsts
    ids = jnp.stack([across, side, me])
    rounded = start_state.astype(bf16)
    code = (element_slot - (me - 1) * slot_count).astype(bf16)
    room = -width % 128
    column = lax.broadcasted_iota(jnp.int32, (elems, room), 1)

    def framed(first_code, second_code):
        extra = jnp.where(column == 0, first_code[:, None], second_code[:, None])
        return jnp.concatenate([rounded, extra], axis=1)

    halo_side = to_side(framed(code, code))
    halo_across = to_across(framed(code, halo_side[:, width]))
    across_live = (across >= 0) & (across < devices)
    nowhere = devices * slot_count
    across_mate = across ^ 1

    def slots_of(codes, home, live):
        return jnp.where(live, codes.astype(jnp.int32) + (home - 1) * slot_count, nowhere)

    first = pl.pallas_call(
        functools.partial(first_kernel, slot_count),
        out_shape=jax.ShapeDtypeStruct((firsts,) + pair, bf16),
        in_specs=[SMEM, SMEM, HBM, HBM, HBM],
        out_specs=HBM,
        scratch_shapes=[pltpu.VMEM((blind,) + block, bf16)] * 2
        + [pltpu.VMEM((firsts,) + pair, bf16), dma((2, blind)), dma((firsts,))],
        compiler_params=ROOMY,
        cost_estimate=SMALL,
        name="first",
    )(element_slot, across[None], pivot_inverse, lower_block, upper_block)
    first, halo_across, halo_side, pivot_inverse, face_blocks = lax.optimization_barrier(
        (first, halo_across, halo_side, pivot_inverse, face_blocks)
    )
    first_in = to_across(first)
    state_side, state_across = halo_side[:, :width], halo_across[:, :width]
    slot_side = slots_of(halo_side[:, width], side, True)
    slot_across = slots_of(halo_across[:, width], across, across_live)
    slot_far = slots_of(halo_across[:, width + 1], across_mate, across_live)
    made = pl.pallas_call(
        functools.partial(rest_kernel, blind, SIDES, slot_count),
        out_shape=[jax.ShapeDtypeStruct((bucket // SIDES,) + pair, bf16)] * SIDES
        + [jax.ShapeDtypeStruct(pair, bf16)] * rests,
        in_specs=[SMEM] * 4 + [HBM] * 3,
        out_specs=[HBM] * (SIDES + rests),
        scratch_shapes=[pltpu.VMEM((2 * rests,) + block, bf16)] * 2
        + [pltpu.VMEM((rests,) + pair, bf16), dma((2, 2 * rests)), dma((rests,))]
        + [pltpu.VMEM((bucket,) + block, bf16)] * 3
        + [pltpu.VMEM((bucket,) + pair, bf16), dma((3, bucket)), dma((bucket,))],
        compiler_params=ROOMY,
        cost_estimate=SMALL,
        name="rest",
    )(element_slot, slot_across, slot_far, ids, pivot_inverse, lower_block, upper_block)
    rest = made[SIDES:]
    side_in = tuple(to_side(part) for part in made[:SIDES])
    whole = jax.ShapeDtypeStruct((slot_count,), jnp.int32)
    some = jax.ShapeDtypeStruct((elems,), jnp.int32)
    table, lower_at, upper_at, back, item_of_own, send_index, counts = pl.pallas_call(
        functools.partial(plan_kernel, blind, slot_count),
        out_shape=[whole] * 4 + [some] * 2 + [jax.ShapeDtypeStruct((2,), jnp.int32)],
        in_specs=[SMEM] * 5,
        out_specs=[SMEM] * 7,
        cost_estimate=SMALL,
        name="plan",
    )(element_slot, slot_side, slot_across, slot_far, ids)

    own_pack = pl.pallas_call(
        functools.partial(staying_kernel, slot_count),
        out_shape=jax.ShapeDtypeStruct((elems,) + pair, bf16),
        in_specs=[SMEM, SMEM, HBM, HBM, HBM],
        out_specs=HBM,
        scratch_shapes=[pltpu.VMEM((elems,) + block, bf16)] * 3
        + [pltpu.VMEM((elems,) + pair, bf16), dma((3, elems)), dma((elems,))],
        compiler_params=ROOMY,
        cost_estimate=SMALL,
        name="staying",
    )(element_slot, me[None], pivot_inverse, lower_block, upper_block)

    home = neighbours // elems
    within = neighbours % elems
    near = jnp.where(home == me, elems, jnp.where(home == side, 0, 2 * elems)) + within
    near = jnp.where(neighbours >= 0, near, -1)
    all_slots = jnp.concatenate([slot_side, element_slot, slot_across])
    place = all_slots[jnp.maximum(near, 0)]
    place_owner = place // slot_count
    place_slot = place % slot_count
    place_row = (place_slot % LMAX) * lines + place_slot // LMAX
    across_chip = across // 2
    far = jnp.where(
        place_owner == me,
        0,
        jnp.where(
            place_owner == side,
            slot_count,
            jnp.where(place_owner // 2 == across_chip, 2 * slot_count, 4 * slot_count)
            + (place_owner % 2) * slot_count,
        ),
    )
    far = jnp.where(neighbours >= 0, far + place_row, -1)

    def face_part(index, parts):
        counts = tuple(part.shape[0] for part in parts)
        return pl.pallas_call(
            functools.partial(face_kernel, counts),
            out_shape=[
                jax.ShapeDtypeStruct((bucket, width), f32),
                jax.ShapeDtypeStruct((bucket, width), f32),
                jax.ShapeDtypeStruct((elems, width), f32),
            ],
            in_specs=[SMEM, VMEM, VMEM] + [VMEM] * len(parts) + [HBM, HBM],
            out_specs=[VMEM] * 3,
            scratch_shapes=[
                pltpu.VMEM((sum(counts), width), bf16),
                pltpu.VMEM((faces * elems, width), f32),
                pltpu.VMEM((128, width + room), f32),
                pltpu.VMEM((width + room, 128), f32),
                pltpu.VMEM((width, 128), bf16),
                pltpu.VMEM((width + room, 128), f32),
                pltpu.VMEM((elems, faces) + block, bf16),
                pltpu.VMEM((elems,) + block, bf16),
                dma((elems,)),
                dma((elems,)),
            ],
            compiler_params=FACING,
            cost_estimate=SMALL,
            name="faces",
        )(send_index, index.reshape(-1, 1), right_side, *parts, face_blocks, pivot_inverse)

    def solve(last, blocks, side_s, own_s, across_s):
        if last:
            shapes = [(bucket, width), (elems, width), (bucket, width)]
            out_shape = [jax.ShapeDtypeStruct(shape, f32) for shape in shapes]
        else:
            out_shape = [jax.ShapeDtypeStruct((slot_count, width), bf16)]
        return pl.pallas_call(
            functools.partial(solve_kernel, last, rests),
            out_shape=out_shape,
            in_specs=[SMEM] * 5 + [HBM] * (SIDES + 2 + rests) + [VMEM] * 3,
            out_specs=[VMEM] * len(out_shape),
            scratch_shapes=[
                pltpu.VMEM((slot_count,) + pair, bf16),
                pltpu.VMEM((slot_count, width), f32),
                pltpu.VMEM((LMAX, 8, width), f32),
                pltpu.VMEM((LMAX, 8, width), f32),
                dma((slot_count,)),
                dma((1,)),
                dma((rests,)),
            ],
            compiler_params=SNUG,
            cost_estimate=SMALL,
            name="solve",
        )(table, lower_at, upper_at, back, counts, *blocks, side_s, own_s, across_s)

    def exchange(going, coming, *arrays):
        *blocks, vectors = arrays
        got = []
        for j, block in enumerate(blocks):
            pairs = (up_pairs if j < going else []) + (down_pairs if j < coming else [])
            if pairs:
                got.append(lax.ppermute(block, "dom", pairs))
        unused = len(blocks) - len(got)
        if unused:
            got += pl.pallas_call(
                nothing_kernel, out_shape=[jax.ShapeDtypeStruct(pair, bf16)] * unused, out_specs=[HBM] * unused, name="unused"
            )()
        return (*got, to_across(vectors))

    exchanges = [
        functools.partial(exchange, going, coming) for going in range(rests + 1) for coming in range(rests + 1)
    ]
    index, parts = near, [state_side, rounded, state_across]
    for sweep in range(SWEEPS):
        scaled_side, scaled_across, scaled_own = face_part(index, parts)
        got_side = to_side(scaled_side)
        if sweep == 0:
            rest, scaled_across, counts, own_pack, first_in, side_in, got_side = lax.optimization_barrier(
                (tuple(rest), scaled_across, counts, own_pack, first_in, side_in, got_side)
            )
            going = jnp.where(odd, counts[0], counts[1])
            coming = jnp.where(odd, counts[1], counts[0])
            branch = going * (rests + 1) + coming
            *rest_in, got_across = lax.switch(branch, exchanges, *rest, scaled_across)
        else:
            got_across = to_across(scaled_across)
        blocks = (*side_in, own_pack, first_in, *rest_in)
        solved = solve(sweep == SWEEPS - 1, blocks, got_side, scaled_own, got_across)
        if sweep < SWEEPS - 1:
            (mine,) = solved
            beside = to_side(mine)
            chip = jnp.where(
                odd, jnp.concatenate([beside, mine]), jnp.concatenate([mine, beside])
            )
            over = to_across(chip)
            under = to_side(over)
            index, parts = far, [mine, beside, over, under]
    back_side, back_own, back_across = solved
    back_across = to_across(back_across)
    back_side = to_side(back_side)
    return pl.pallas_call(
        place_kernel,
        out_shape=jax.ShapeDtypeStruct((elems, width), f32),
        in_specs=[SMEM, VMEM, VMEM, VMEM],
        out_specs=VMEM,
        scratch_shapes=[pltpu.VMEM((slot_count, width), f32)],
        name="place",
    )(item_of_own, back_side, back_own, back_across)


def solution(mesh):
    placed = (
        P("dom", None),
        P("dom", None),
        P("dom", None, None),
        P("dom", None, None),
        P("dom", None, None),
        P("dom", None, None, None),
        P(None, "dom"),
        P("dom"),
    )
    return jax.shard_map(
        body, mesh=mesh, in_specs=placed, out_specs=P("dom", None), check_vma=False
    )
```

```python
import functools

import jax
import jax.numpy as jnp
from jax import lax
from jax.experimental import pallas as pl
from jax.experimental.pallas import tpu as pltpu
from jax.sharding import PartitionSpec as P

LMAX = 8
FIRST = 4
SIDES = 4
SWEEPS = 2
WIDE = 256
HBM = pl.BlockSpec(memory_space=pltpu.HBM)
SMEM = pl.BlockSpec(memory_space=pltpu.SMEM)
VMEM = pl.BlockSpec(memory_space=pltpu.VMEM)
ROOMY = pltpu.CompilerParams(vmem_limit_bytes=57 << 20)
FACING = pltpu.CompilerParams(vmem_limit_bytes=50 << 20)
SNUG = pltpu.CompilerParams(vmem_limit_bytes=52 << 20)
PLAIN = pltpu.CompilerParams(vmem_limit_bytes=16 << 20)
SMALL = pl.CostEstimate(flops=1 << 20, bytes_accessed=1 << 20, transcendentals=0)
NT = (((1,), (1,)), ((), ()))


def dot_nt(a, b):
    return lax.dot_general(a, b, NT, preferred_element_type=jnp.float32)


def dot_nn(a, b):
    return jnp.dot(a, b, preferred_element_type=jnp.float32)


def put_pair(first, second, out):
    out[:, :WIDE] = first[:, :WIDE]
    out[:, WIDE : 2 * WIDE] = second[:, :WIDE]
    out[:, 2 * WIDE :] = jnp.concatenate([first[:, WIDE:], second[:, WIDE:]], axis=1)


def pair_product(pivot, lower, upper, out):
    both = jnp.concatenate([lower.T, upper.T], axis=0)
    got = dot_nt(both, pivot).astype(jnp.bfloat16)
    width = pivot.shape[0]
    put_pair(got[:width], got[width:], out)


def places_taken(slots, owner, slot_count, taken):
    for e in range(slots.shape[0]):
        mine = slots[e] // slot_count == owner
        taken = jnp.where(mine, taken | (jnp.int32(1) << (slots[e] % slot_count)), taken)
    return taken


def is_taken(taken, slot):
    return ((taken >> slot) & 1) == 1


def block_jobs(slot, taken, hit, blind, seen, extra):
    jobs = []
    position = slot % LMAX
    for possible, beside in ((position > 0, slot - 1), (position < LMAX - 1, slot + 1)):
        possible = hit & possible
        early = possible & (seen < blind)
        late = possible & (seen >= blind) & is_taken(taken, jnp.clip(beside, 0, 31))
        jobs.append((early, late, seen, extra))
        seen = seen + possible.astype(jnp.int32)
        extra = extra + late.astype(jnp.int32)
    return jobs, seen, extra


def run_jobs(count, piv, pb, mb, stage, outs, insem, outsem):
    def pair_copies(at):
        return [pltpu.make_async_copy(stage.at[at], out, outsem.at[at]) for out in outs]

    def step(j, carry):
        def arrived(m):
            pltpu.make_async_copy(piv.at[0], pb.at[m], insem.at[0, m]).wait()
            pltpu.make_async_copy(piv.at[0], mb.at[m], insem.at[1, m]).wait()

        arrived(2 * j)

        @pl.when(2 * j + 1 < count)
        def _():
            arrived(2 * j + 1)

        first, second = [dot_nt(mb[m].T, pb[m]).astype(jnp.bfloat16) for m in (2 * j, 2 * j + 1)]
        put_pair(first, second, stage.at[j])
        for i, copy in enumerate(pair_copies(j)):

            @pl.when(j == i)
            def _(copy=copy):
                copy.start()

        return carry

    lax.fori_loop(0, (count + 1) // 2, step, 0)
    for j in range(len(outs)):

        @pl.when(2 * j < count)
        def _(j=j):
            pltpu.make_async_copy(stage.at[j], outs[j], outsem.at[j]).wait()


def first_kernel(slot_count, slots, across, piv, low, upp, out, pb, mb, stage, insem, outsem):
    blind = 2 * out.shape[0]
    seen, extra = jnp.int32(0), jnp.int32(0)
    for e in range(slots.shape[0]):
        hit = slots[e] // slot_count == across[0]
        jobs, seen, extra = block_jobs(slots[e] % slot_count, jnp.int32(0), hit, blind, seen, extra)
        for (early, _, at, _), source in zip(jobs, (low, upp)):

            @pl.when(early)
            def _(e=e, at=at, source=source):
                pltpu.make_async_copy(piv.at[e], pb.at[at], insem.at[0, at]).start()
                pltpu.make_async_copy(source.at[e], mb.at[at], insem.at[1, at]).start()

    outs = [out.at[j] for j in range(out.shape[0])]
    run_jobs(jnp.minimum(seen, blind), piv, pb, mb, stage, outs, insem, outsem)


def rest_kernel(blind, sides, slot_count, slots, across_slots, far_slots, ids, piv, low, upp, *refs):
    side_outs, refs = refs[:sides], refs[sides:]
    outs = refs[: len(refs) - 11]
    share = side_outs[0].shape[0]
    pb, mb, stage, insem, outsem, sp, sl, su, side_stage, side_in, side_sem = refs[len(outs) :]
    across, side = ids[0], ids[1]
    taken = jnp.int32(0)
    for array in (slots, across_slots, far_slots):
        taken = places_taken(array, across, slot_count, taken)
    seen, extra, beside = jnp.int32(0), jnp.int32(0), jnp.int32(0)
    for e in range(slots.shape[0]):
        owner = slots[e] // slot_count
        jobs, seen, extra = block_jobs(slots[e] % slot_count, taken, owner == across, blind, seen, extra)
        for (_, late, _, at), source in zip(jobs, (low, upp)):

            @pl.when(late)
            def _(e=e, at=at, source=source):
                pltpu.make_async_copy(piv.at[e], pb.at[at], insem.at[0, at]).start()
                pltpu.make_async_copy(source.at[e], mb.at[at], insem.at[1, at]).start()

    for e in range(slots.shape[0]):
        hit = slots[e] // slot_count == side

        @pl.when(hit)
        def _(e=e, beside=beside):
            pltpu.make_async_copy(piv.at[e], sp.at[beside], side_in.at[0, beside]).start()
            pltpu.make_async_copy(low.at[e], sl.at[beside], side_in.at[1, beside]).start()
            pltpu.make_async_copy(upp.at[e], su.at[beside], side_in.at[2, beside]).start()

        beside = beside + hit.astype(jnp.int32)
    run_jobs(extra, piv, pb, mb, stage, outs, insem, outsem)

    def step(k, carry):
        pltpu.make_async_copy(piv.at[0], sp.at[k], side_in.at[0, k]).wait()
        pltpu.make_async_copy(piv.at[0], sl.at[k], side_in.at[1, k]).wait()
        pltpu.make_async_copy(piv.at[0], su.at[k], side_in.at[2, k]).wait()
        pair_product(sp[k], sl[k], su[k], side_stage.at[k])
        for j, side_out in enumerate(side_outs):

            @pl.when(k // share == j)
            def _(side_out=side_out):
                pltpu.make_async_copy(side_stage.at[k], side_out.at[k % share], side_sem.at[k]).start()

        return carry

    def drain(k, carry):
        pltpu.make_async_copy(side_stage.at[k], side_outs[0].at[0], side_sem.at[k]).wait()
        return carry

    lax.fori_loop(0, beside, step, 0)
    lax.fori_loop(0, beside, drain, 0)


def plan_kernel(blind, slot_count, slots, side_slots, across_slots, far_slots, ids, table, lower_at, upper_at, back, item_of_own, send, counts):
    across, side, me = ids[0], ids[1], ids[2]
    elems = slots.shape[0]
    bucket = elems // 2
    for k in range(slot_count):
        table[k] = jnp.int32(-1)
        lower_at[k] = jnp.int32(-1)
        upper_at[k] = jnp.int32(-1)
        back[k] = jnp.int32(0)
    for k in range(2 * bucket):
        send[k] = jnp.int32(0)
    taken, beyond = jnp.int32(0), jnp.int32(0)
    for array in (slots, side_slots, across_slots):
        taken = places_taken(array, me, slot_count, taken)
    for array in (slots, across_slots, far_slots):
        beyond = places_taken(array, across, slot_count, beyond)
    beside, over = jnp.int32(0), jnp.int32(0)
    seen, out_extra = jnp.int32(0), jnp.int32(0)
    for e in range(elems):
        owner, slot = slots[e] // slot_count, slots[e] % slot_count
        own, to_side, to_across = owner == me, owner == side, owner == across
        item_of_own[e] = jnp.where(own, bucket + e, jnp.where(to_side, beside, bucket + elems + over))

        @pl.when(own)
        def _(e=e, slot=slot):
            table[slot] = jnp.int32(bucket + e)
            lower_at[slot] = jnp.int32(2 * (bucket + e))
            upper_at[slot] = jnp.int32(2 * (bucket + e) + 1)
            back[bucket + e] = slot

        @pl.when(to_side)
        def _(e=e, beside=beside):
            send[beside] = jnp.int32(e)

        @pl.when(to_across)
        def _(e=e, over=over):
            send[bucket + over] = jnp.int32(e)

        _, seen, out_extra = block_jobs(slot, beyond, to_across, blind, seen, out_extra)
        beside = beside + to_side.astype(jnp.int32)
        over = over + to_across.astype(jnp.int32)
    k = jnp.int32(0)
    for e in range(elems):
        mine, slot = side_slots[e] // slot_count == me, side_slots[e] % slot_count

        @pl.when(mine)
        def _(k=k, slot=slot):
            table[slot] = k
            lower_at[slot] = 2 * k
            upper_at[slot] = 2 * k + 1
            back[k] = slot

        k = k + mine.astype(jnp.int32)
    k = jnp.int32(bucket + elems)
    seen, in_extra = jnp.int32(0), jnp.int32(0)
    for e in range(elems):
        mine, slot = across_slots[e] // slot_count == me, across_slots[e] % slot_count
        jobs, seen, in_extra = block_jobs(slot, taken, mine, blind, seen, in_extra)

        @pl.when(mine)
        def _(k=k, slot=slot, jobs=jobs):
            table[slot] = k
            back[k] = slot
            for (early, late, first, extra), at in zip(jobs, (lower_at, upper_at)):
                place = jnp.where(early, first, jnp.where(late, blind + extra, jnp.int32(-1)))
                at[slot] = jnp.where(place >= 0, place + 2 * (bucket + elems), place)

        k = k + mine.astype(jnp.int32)
    counts[0] = (out_extra + 1) // 2
    counts[1] = (in_extra + 1) // 2


def staying_kernel(slot_count, slots, me, piv, low, upp, own, pb, lb, ub, stage, insem, outsem):
    elems = slots.shape[0]

    def loads(e):
        return [
            pltpu.make_async_copy(src.at[e], dst.at[e], insem.at[i, e])
            for i, (src, dst) in enumerate(((piv, pb), (low, lb), (upp, ub)))
        ]

    def send(e):
        return pltpu.make_async_copy(stage.at[e], own.at[e], outsem.at[e])

    for e in range(elems):

        @pl.when(slots[e] // slot_count == me[0])
        def _(e=e):
            for copy in loads(e):
                copy.start()

    def step(e, carry):
        @pl.when(slots[e] // slot_count == me[0])
        def _():
            for copy in loads(e):
                copy.wait()
            pair_product(pb[e], lb[e], ub[e], stage.at[e])
            send(e).start()

        return carry

    lax.fori_loop(0, elems, step, 0)
    for e in range(elems):

        @pl.when(slots[e] // slot_count == me[0])
        def _(e=e):
            send(e).wait()


def face_kernel(counts, send, index, rhs, *refs):
    parts = refs[: len(counts)]
    faces, piv, side_out, across_out, own_out, rows, gathered, flat, rhs_t, held, scaled, fb, pb, fsem, psem = refs[
        len(counts) :
    ]
    elems, width = rhs.shape
    count = faces.shape[1]
    for e in range(elems):
        pltpu.make_async_copy(faces.at[e], fb.at[e], fsem.at[e]).start()
        pltpu.make_async_copy(piv.at[e], pb.at[e], psem.at[e]).start()
    at = 0
    for part, size in zip(parts, counts):
        rows[at : at + size] = part[...]
        at += size
    wanted = index[...] == lax.broadcasted_iota(jnp.int32, (count * elems, at), 1)
    gathered[...] = dot_nn(wanted.astype(jnp.bfloat16), rows[...])
    flat[...] = jnp.zeros(flat.shape, jnp.float32)
    flat[:elems, :width] = rhs[...]
    rhs_t[...] = flat[...].T
    lanes = rhs_t.shape[1]
    column = lax.broadcasted_iota(jnp.int32, (width, lanes), 1)

    def residual(e):
        pltpu.make_async_copy(faces.at[e], fb.at[e], fsem.at[e]).wait()
        states = [gathered[pl.ds(f * elems + e, 1), :] for f in range(count)]

        def term(f, low, high):
            return fb[e, f, :, low:high].astype(jnp.float32) * states[f][:, low:high]

        lead, ending = None, None
        for f in range(count):
            for low in range(0, WIDE, lanes):
                more = term(f, low, low + lanes)
                lead = more if lead is None else lead + more
            more = term(f, WIDE, width)
            ending = more if ending is None else ending + more
        total = jnp.sum(lead, axis=1, keepdims=True) + jnp.sum(ending, axis=1, keepdims=True)
        return (rhs_t[:width] - total).astype(jnp.bfloat16)

    def apply(e):
        pltpu.make_async_copy(piv.at[e], pb.at[e], psem.at[e]).wait()
        scaled[:width] = jnp.where(column == e, dot_nn(pb[e], held[...]), scaled[:width])

    scaled[...] = jnp.zeros(scaled.shape, jnp.float32)
    held[...] = residual(0)

    def step(e, carry):
        apply(e - 1)
        held[...] = residual(e)
        return carry

    lax.fori_loop(1, elems, step, 0)
    apply(elems - 1)
    flat[...] = scaled[...].T
    own_out[...] = flat[:elems, :width]
    bucket = side_out.shape[0]
    for k in range(bucket):
        side_out[k : k + 1] = flat[pl.ds(send[k], 1), :][:, :width]
        across_out[k : k + 1] = flat[pl.ds(send[bucket + k], 1), :][:, :width]


def solve_kernel(last, rests, table, lower_at, upper_at, back, counts, *refs):
    sides_m, (own_m, first_m), refs = refs[:SIDES], refs[SIDES : SIDES + 2], refs[SIDES + 2 :]
    rest_m = refs[:rests]
    side_s, own_s, across_s = refs[rests : rests + 3]
    refs = refs[rests + 3 :]
    outs = refs[:3] if last else refs[:1]
    mats, items, ahead, behind, sems, first_sem, rest_sem = refs[len(outs) :]
    bucket = side_s.shape[0]
    elems = own_s.shape[0]
    width = own_s.shape[1]
    lines = table.shape[0] // LMAX
    tail = width - WIDE
    firsts = first_m.shape[0]
    base = bucket + elems
    first_copy = pltpu.make_async_copy(first_m, mats.at[base : base + firsts], first_sem.at[0])
    first_copy.start()
    rest_copies = [
        pltpu.make_async_copy(rest, mats.at[base + firsts + j], rest_sem.at[j]) for j, rest in enumerate(rest_m)
    ]
    for j, copy in enumerate(rest_copies):

        @pl.when(j < counts[1])
        def _(copy=copy):
            copy.start()

    share = bucket // SIDES
    sources = [(side_m, j * share, (j + 1) * share) for j, side_m in enumerate(sides_m)] + [(own_m, bucket, base)]
    for p in range(LMAX):
        for r in range(lines):
            item = table[r * LMAX + p]
            for source, low, high in sources:

                @pl.when((item >= low) & (item < high))
                def _(source=source, low=low, item=item, p=p, r=r):
                    sem = sems.at[p * lines + r]
                    pltpu.make_async_copy(source.at[item - low], mats.at[item], sem).start()

    items[:bucket] = side_s[...]
    items[bucket : bucket + elems] = own_s[...]
    items[bucket + elems :] = across_s[...]
    sublanes = ahead.shape[1]
    row = lax.broadcasted_iota(jnp.int32, (sublanes, width), 0)

    def sweep_step(p, x, places):
        carried = jnp.zeros((sublanes, width), jnp.float32)
        for r in range(lines):
            place = places[r * LMAX + p]
            at = jnp.maximum(place, 0)
            unit, half = at // 2, at % 2
            lead = dot_nn(x, mats[unit, :, pl.ds(pl.multiple_of(half * WIDE, WIDE), WIDE)])
            ending = dot_nn(x, mats[unit, :, 2 * WIDE :])
            ending = jnp.where(half == 0, ending[:, :tail], ending[:, tail:])
            carried = jnp.where((row == r) & (place >= 0), jnp.concatenate([lead, ending], axis=1), carried)
        return carried

    for p in range(LMAX):
        ahead[p] = jnp.zeros((sublanes, width), jnp.float32)
        for r in range(lines):
            item = table[r * LMAX + p]

            @pl.when(item >= 0)
            def _(p=p, r=r, item=item):
                ahead[p, r : r + 1, :] = items[pl.ds(item, 1), :]

    x = None
    for p in range(LMAX):
        for r in range(lines):

            item = table[r * LMAX + p]

            @pl.when((item >= 0) & (item < base))
            def _(p=p, r=r, item=item):
                pltpu.make_async_copy(own_m.at[0], mats.at[item], sems.at[p * lines + r]).wait()

        if p == 1:
            first_copy.wait()
            for j, copy in enumerate(rest_copies):

                @pl.when(j < counts[1])
                def _(copy=copy):
                    copy.wait()

        value = ahead[p]
        if p > 0:
            value = value - sweep_step(p, x, lower_at)
            ahead[p] = value
        x = value.astype(jnp.bfloat16)
    x = None
    for p in reversed(range(LMAX)):
        value = ahead[p]
        if p < LMAX - 1:
            value = value - sweep_step(p, x, upper_at)
        behind[p] = value
        x = value.astype(jnp.bfloat16)
    if last:
        at = 0
        for out in outs:
            for k in range(out.shape[0]):
                slot = back[at + k]
                out[k : k + 1] = behind[slot % LMAX, pl.ds(slot // LMAX, 1), :]
            at += out.shape[0]
    else:
        (out,) = outs
        for p in range(LMAX):
            items[p * lines : (p + 1) * lines] = behind[p, :lines, :]
        out[...] = items[...].astype(jnp.bfloat16)


def nothing_kernel(*outs):
    pass


def place_kernel(index, side, own, across, out, items):
    bucket = side.shape[0]
    elems = own.shape[0]
    items[:bucket] = side[...]
    items[bucket : bucket + elems] = own[...]
    items[bucket + elems :] = across[...]
    for e in range(elems):
        out[e : e + 1] = items[pl.ds(index[e], 1), :]


def body(
    right_side,
    start_state,
    pivot_inverse,
    lower_block,
    upper_block,
    face_blocks,
    neighbours,
    element_slot,
):
    elems, width = right_side.shape
    faces = face_blocks.shape[1]
    bucket = elems // 2
    slot_count = 2 * elems
    lines = slot_count // LMAX
    packed = 2 * width
    devices = lax.axis_size("dom")
    me = lax.axis_index("dom").astype(jnp.int32)
    odd = me % 2 == 1
    side = jnp.where(odd, me - 1, me + 1)
    across = jnp.where(odd, me + 1, me - 1)
    side_pairs = [(i, i ^ 1) for i in range(devices)]
    up_pairs = [(i, i + 1) for i in range(1, devices - 1, 2)]
    down_pairs = [(j, i) for i, j in up_pairs]
    across_pairs = up_pairs + down_pairs

    def to_side(array):
        return lax.ppermute(array, "dom", side_pairs)

    def to_across(array):
        return lax.ppermute(array, "dom", across_pairs)

    f32, bf16 = jnp.float32, jnp.bfloat16
    block = (width, width)
    pair = (width, packed)
    dma = pltpu.SemaphoreType.DMA

    firsts, rests = FIRST, bucket - FIRST
    blind = 2 * firsts
    ids = jnp.stack([across, side, me])
    rounded = start_state.astype(bf16)
    code = (element_slot - (me - 1) * slot_count).astype(bf16)
    room = -width % 128
    column = lax.broadcasted_iota(jnp.int32, (elems, room), 1)

    def framed(first_code, second_code):
        extra = jnp.where(column == 0, first_code[:, None], second_code[:, None])
        return jnp.concatenate([rounded, extra], axis=1)

    halo_side = to_side(framed(code, code))
    halo_across = to_across(framed(code, halo_side[:, width]))
    across_live = (across >= 0) & (across < devices)
    nowhere = devices * slot_count
    across_mate = across ^ 1

    def slots_of(codes, home, live):
        return jnp.where(live, codes.astype(jnp.int32) + (home - 1) * slot_count, nowhere)

    first = pl.pallas_call(
        functools.partial(first_kernel, slot_count),
        out_shape=jax.ShapeDtypeStruct((firsts,) + pair, bf16),
        in_specs=[SMEM, SMEM, HBM, HBM, HBM],
        out_specs=HBM,
        scratch_shapes=[pltpu.VMEM((blind,) + block, bf16)] * 2
        + [pltpu.VMEM((firsts,) + pair, bf16), dma((2, blind)), dma((firsts,))],
        compiler_params=ROOMY,
        cost_estimate=SMALL,
        name="first",
    )(element_slot, across[None], pivot_inverse, lower_block, upper_block)
    pivot_inverse, lower_block, upper_block, face_blocks = [
        pltpu.with_memory_space_constraint(array, pltpu.HBM)
        for array in (pivot_inverse, lower_block, upper_block, face_blocks)
    ]
    first, halo_across, halo_side, pivot_inverse, face_blocks = lax.optimization_barrier(
        (first, halo_across, halo_side, pivot_inverse, face_blocks)
    )
    first_in = to_across(first)
    state_side, state_across = halo_side[:, :width], halo_across[:, :width]
    slot_side = slots_of(halo_side[:, width], side, True)
    slot_across = slots_of(halo_across[:, width], across, across_live)
    slot_far = slots_of(halo_across[:, width + 1], across_mate, across_live)
    made = pl.pallas_call(
        functools.partial(rest_kernel, blind, SIDES, slot_count),
        out_shape=[jax.ShapeDtypeStruct((bucket // SIDES,) + pair, bf16)] * SIDES
        + [jax.ShapeDtypeStruct(pair, bf16)] * rests,
        in_specs=[SMEM] * 4 + [HBM] * 3,
        out_specs=[HBM] * (SIDES + rests),
        scratch_shapes=[pltpu.VMEM((2 * rests,) + block, bf16)] * 2
        + [pltpu.VMEM((rests,) + pair, bf16), dma((2, 2 * rests)), dma((rests,))]
        + [pltpu.VMEM((bucket,) + block, bf16)] * 3
        + [pltpu.VMEM((bucket,) + pair, bf16), dma((3, bucket)), dma((bucket,))],
        compiler_params=ROOMY,
        cost_estimate=SMALL,
        name="rest",
    )(element_slot, slot_across, slot_far, ids, pivot_inverse, lower_block, upper_block)
    rest = made[SIDES:]
    side_in = tuple(to_side(part) for part in made[:SIDES])
    whole = jax.ShapeDtypeStruct((slot_count,), jnp.int32)
    some = jax.ShapeDtypeStruct((elems,), jnp.int32)
    table, lower_at, upper_at, back, item_of_own, send_index, counts = pl.pallas_call(
        functools.partial(plan_kernel, blind, slot_count),
        out_shape=[whole] * 4 + [some] * 2 + [jax.ShapeDtypeStruct((2,), jnp.int32)],
        in_specs=[SMEM] * 5,
        out_specs=[SMEM] * 7,
        compiler_params=PLAIN,
        cost_estimate=SMALL,
        name="plan",
    )(element_slot, slot_side, slot_across, slot_far, ids)

    own_pack = pl.pallas_call(
        functools.partial(staying_kernel, slot_count),
        out_shape=jax.ShapeDtypeStruct((elems,) + pair, bf16),
        in_specs=[SMEM, SMEM, HBM, HBM, HBM],
        out_specs=HBM,
        scratch_shapes=[pltpu.VMEM((elems,) + block, bf16)] * 3
        + [pltpu.VMEM((elems,) + pair, bf16), dma((3, elems)), dma((elems,))],
        compiler_params=ROOMY,
        cost_estimate=SMALL,
        name="staying",
    )(element_slot, me[None], pivot_inverse, lower_block, upper_block)

    home = neighbours // elems
    within = neighbours % elems
    near = jnp.where(home == me, elems, jnp.where(home == side, 0, 2 * elems)) + within
    near = jnp.where(neighbours >= 0, near, -1)
    all_slots = jnp.concatenate([slot_side, element_slot, slot_across])
    place = all_slots[jnp.maximum(near, 0)]
    place_owner = place // slot_count
    place_slot = place % slot_count
    place_row = (place_slot % LMAX) * lines + place_slot // LMAX
    across_chip = across // 2
    far = jnp.where(
        place_owner == me,
        0,
        jnp.where(
            place_owner == side,
            slot_count,
            jnp.where(place_owner // 2 == across_chip, 2 * slot_count, 4 * slot_count)
            + (place_owner % 2) * slot_count,
        ),
    )
    far = jnp.where(neighbours >= 0, far + place_row, -1)

    def face_part(index, parts):
        counts = tuple(part.shape[0] for part in parts)
        return pl.pallas_call(
            functools.partial(face_kernel, counts),
            out_shape=[
                jax.ShapeDtypeStruct((bucket, width), f32),
                jax.ShapeDtypeStruct((bucket, width), f32),
                jax.ShapeDtypeStruct((elems, width), f32),
            ],
            in_specs=[SMEM, VMEM, VMEM] + [VMEM] * len(parts) + [HBM, HBM],
            out_specs=[VMEM] * 3,
            scratch_shapes=[
                pltpu.VMEM((sum(counts), width), bf16),
                pltpu.VMEM((faces * elems, width), f32),
                pltpu.VMEM((128, width + room), f32),
                pltpu.VMEM((width + room, 128), f32),
                pltpu.VMEM((width, 128), bf16),
                pltpu.VMEM((width + room, 128), f32),
                pltpu.VMEM((elems, faces) + block, bf16),
                pltpu.VMEM((elems,) + block, bf16),
                dma((elems,)),
                dma((elems,)),
            ],
            compiler_params=FACING,
            cost_estimate=SMALL,
            name="faces",
        )(send_index, index.reshape(-1, 1), right_side, *parts, face_blocks, pivot_inverse)

    def solve(last, blocks, side_s, own_s, across_s):
        if last:
            shapes = [(bucket, width), (elems, width), (bucket, width)]
            out_shape = [jax.ShapeDtypeStruct(shape, f32) for shape in shapes]
        else:
            out_shape = [jax.ShapeDtypeStruct((slot_count, width), bf16)]
        return pl.pallas_call(
            functools.partial(solve_kernel, last, rests),
            out_shape=out_shape,
            in_specs=[SMEM] * 5 + [HBM] * (SIDES + 2 + rests) + [VMEM] * 3,
            out_specs=[VMEM] * len(out_shape),
            scratch_shapes=[
                pltpu.VMEM((slot_count,) + pair, bf16),
                pltpu.VMEM((slot_count, width), f32),
                pltpu.VMEM((LMAX, 8, width), f32),
                pltpu.VMEM((LMAX, 8, width), f32),
                dma((slot_count,)),
                dma((1,)),
                dma((rests,)),
            ],
            compiler_params=SNUG,
            cost_estimate=SMALL,
            name="solve",
        )(table, lower_at, upper_at, back, counts, *blocks, side_s, own_s, across_s)

    def exchange(going, coming, *arrays):
        *blocks, vectors = arrays
        got = []
        for j, block in enumerate(blocks):
            pairs = (up_pairs if j < going else []) + (down_pairs if j < coming else [])
            if pairs:
                got.append(lax.ppermute(block, "dom", pairs))
        unused = len(blocks) - len(got)
        if unused:
            got += pl.pallas_call(
                nothing_kernel,
                out_shape=[jax.ShapeDtypeStruct(pair, bf16)] * unused,
                out_specs=[HBM] * unused,
                compiler_params=PLAIN,
                name="unused",
            )()
        return (*got, to_across(vectors))

    exchanges = [
        functools.partial(exchange, going, coming) for going in range(rests + 1) for coming in range(rests + 1)
    ]
    index, parts = near, [state_side, rounded, state_across]
    for sweep in range(SWEEPS):
        scaled_side, scaled_across, scaled_own = face_part(index, parts)
        got_side = to_side(scaled_side)
        if sweep == 0:
            rest, scaled_across, counts, own_pack, first_in, side_in, got_side = lax.optimization_barrier(
                (tuple(rest), scaled_across, counts, own_pack, first_in, side_in, got_side)
            )
            going = jnp.where(odd, counts[0], counts[1])
            coming = jnp.where(odd, counts[1], counts[0])
            branch = going * (rests + 1) + coming
            *rest_in, got_across = lax.switch(branch, exchanges, *rest, scaled_across)
        else:
            got_across = to_across(scaled_across)
        blocks = (*side_in, own_pack, first_in, *rest_in)
        solved = solve(sweep == SWEEPS - 1, blocks, got_side, scaled_own, got_across)
        if sweep < SWEEPS - 1:
            (mine,) = solved
            beside = to_side(mine)
            chip = jnp.where(
                odd, jnp.concatenate([beside, mine]), jnp.concatenate([mine, beside])
            )
            over = to_across(chip)
            under = to_side(over)
            index, parts = far, [mine, beside, over, under]
    back_side, back_own, back_across = solved
    back_across = to_across(back_across)
    back_side = to_side(back_side)
    return pl.pallas_call(
        place_kernel,
        out_shape=jax.ShapeDtypeStruct((elems, width), f32),
        in_specs=[SMEM, VMEM, VMEM, VMEM],
        out_specs=VMEM,
        scratch_shapes=[pltpu.VMEM((slot_count, width), f32)],
        compiler_params=PLAIN,
        name="place",
    )(item_of_own, back_side, back_own, back_across)


def solution(mesh):
    placed = (
        P("dom", None),
        P("dom", None),
        P("dom", None, None),
        P("dom", None, None),
        P("dom", None, None),
        P("dom", None, None, None),
        P(None, "dom"),
        P("dom"),
    )
    return jax.shard_map(
        body, mesh=mesh, in_specs=placed, out_specs=P("dom", None), check_vma=False
    )
```
